32 devices in a mesh: stretch: 4 (over y, x), ctx: 8 (over z, core).
Axes of the slice: x: 2, y: 2, z: 4, core: 2. Of those that a mesh axis runs over, the one named last changes fastest.
Arguments:
- post_gate: bfloat16 [4096, 8192], P(('stretch', 'ctx')), may hold values from -6 to 6
- pre_gate: bfloat16 [4096, 8192], P(('stretch', 'ctx')), may hold values from -6 to 6
- values: bfloat16 [4096, 8192], P(('stretch', 'ctx')), may hold values from -6 to 6
- filters: float32 [256, 4096], P('ctx'), may hold values from -0.09375 to 0.09375
- skip_bias: float32 [8192], P('ctx'), may hold values from -1 to 1
- doc_blocks: int32 [16], replicated, may hold values from 1 to 12, 32 in all
Outputs:
- output: bfloat16 [4096, 8192], P(('stretch', 'ctx'))
The draws below stay inside these ranges and needn't reach their ends.
Inputs may be any that keep to these rules, and one draw needn't show every extreme that they name: doc_blocks sum to 32; the largest is exactly 12.
All inputs are finite; a program needn't handle non-finite values.
Results may differ from the reference program's by a relative error of at most 0.0057.
Values may be sent and summed in bfloat16 or wider, within the bound.
A program may use at most 128 MiB of HBM per device.

```python
import math
import jax
import jax.numpy as jnp
import numpy as np
from jax import lax

D = 8192
GROUPS = 256
FLEN = 4096
BLK = 128
NDOC = 16
TOKENS = 4096
MAXB = 12


def block_levels(key, shape, split, low, high):
    def one(dim, blocks):
        heights = jax.random.uniform(jax.random.fold_in(jax.random.fold_in(key, 6), dim), (blocks,), jnp.float32, low / len(split), high / len(split))
        return jnp.repeat(jnp.exp(heights), shape[dim] // blocks).reshape((-1,) + (1,) * (len(shape) - dim - 1))

    factor_of = one(*split[0])
    for cut in split[1:]:
        factor_of = factor_of * one(*cut)
    return factor_of


def profile(amount, total, bound, skew):
    weights = [(1 << 20) // math.isqrt(rank ** skew) + 1 for rank in range(2, amount + 1)]
    rest, given = total - bound - (amount - 1), [1] * (amount - 1)
    while rest > 0:
        movable = [i for i in range(amount - 1) if given[i] < bound]
        mass, left = sum([weights[i] for i in movable]), rest
        for i in movable:
            addition = min(bound - given[i], max(1, left * weights[i] // mass), rest)
            given[i] = given[i] + addition
            rest = rest - addition
    return np.array([bound] + given)


def uneven_parts(key, number_of, total, bound, slope):
    if number_of == 2:
        one = jax.random.randint(key, (), max(1, total - bound), min(bound, total - 1) + 1)
        return jnp.stack([one, total - one])
    tallies = jnp.asarray(profile(number_of, total, bound, slope), jnp.int32)
    pairs = (number_of - 1) // 2
    source_of, receiver = tallies[1:1 + 2 * pairs:2], tallies[2:2 + 2 * pairs:2]
    margin = jnp.minimum(source_of - 1, bound - receiver)
    passed = jax.random.randint(jax.random.fold_in(key, 1), (pairs,), 0, 1 << 20) % (margin + 1)
    tallies = tallies.at[1:1 + 2 * pairs:2].set(source_of - passed).at[2:2 + 2 * pairs:2].set(receiver + passed)
    return tallies[jax.random.permutation(jax.random.fold_in(key, 2), number_of)]


def noise(own_key, dims, deviation, reach, cuts=(), kind=jnp.bfloat16):
    result = jax.random.normal(own_key, dims, jnp.float32) * deviation
    if len(cuts) > 0:
        result = block_levels(own_key, dims, cuts, -0.22, 0.18) * result
    return jnp.clip(result, min=-reach, max=reach).astype(kind)


def setup_inputs(seed: int = 0) -> dict:
    seeds = jax.random.split(jax.random.key(seed), 7)
    return {
        "post_gate": noise(seeds[0], (TOKENS, D), 1.0, 6.0, ((0, 32),)),
        "pre_gate": noise(seeds[1], (TOKENS, D), 1.0, 6.0, ((0, 32),)),
        "values": noise(seeds[2], (TOKENS, D), 1.0, 6.0, ((0, 32),)),
        "filters": noise(seeds[3], (GROUPS, FLEN), FLEN ** -0.5, 0.09375, ((0, 8),), jnp.float32),
        "skip_bias": jnp.clip(jax.random.uniform(seeds[4], (D,), jnp.float32, -1.0, 1.0) * block_levels(seeds[4], (D,), ((0, 8),), -0.4, 0.0), -1.0, 1.0),
        "doc_blocks": uneven_parts(seeds[5], NDOC, TOKENS // BLK, MAXB, 2).astype(jnp.int32),
    }


def block_starts(doc_blocks, block_ids):
    doc_ends = jnp.cumsum(doc_blocks)
    before = doc_ends[None, :] <= block_ids[:, None]
    return jnp.sum(jnp.where(before, doc_blocks[None, :], 0), axis=1)


def reference(post_gate, pre_gate, values, filters, skip_bias, doc_blocks):
    tokens = post_gate.shape[0]
    all_blocks = tokens // BLK
    lag_blocks = FLEN // BLK + 1
    group_width = D // GROUPS
    gated = (pre_gate.astype(jnp.float32) * values.astype(jnp.float32)).astype(jnp.bfloat16)
    block_ids = jnp.arange(all_blocks, dtype=jnp.int32)
    starts = block_starts(doc_blocks, block_ids)
    lag_ids = jnp.arange(lag_blocks, dtype=jnp.int32)
    sources = block_ids[:, None] - lag_ids[None, :]
    live_pairs = (sources >= starts[:, None]).astype(jnp.float32)
    row_ids = jnp.arange(BLK, dtype=jnp.int32)
    tap_index = lag_ids[None, :, None] * BLK + row_ids[:, None, None] - row_ids[None, None, :]
    inside = (tap_index >= 0) & (tap_index < FLEN)
    clipped = jnp.clip(tap_index, 0, FLEN - 1)
    padded = jnp.concatenate([jnp.zeros((FLEN, D), gated.dtype), gated], axis=0)
    grouped = padded.reshape(tokens + FLEN, GROUPS, group_width).transpose(1, 0, 2)

    def one_group(item):
        filter_row, column = item
        kernel = jnp.where(inside, filter_row[clipped], 0.0).astype(jnp.float32)
        blocks = column.reshape(all_blocks + lag_blocks - 1, BLK, group_width)
        window = jnp.stack([blocks[lag_blocks - 1 - lag_step: lag_blocks - 1 - lag_step + all_blocks] for lag_step in range(lag_blocks)], axis=1)
        window = window.astype(jnp.float32) * live_pairs[:, :, None, None]
        return jnp.einsum("rjs,ijsw->irw", kernel, window, precision=lax.Precision.HIGHEST)

    conv = lax.map(one_group, (filters, grouped))
    conv = conv.transpose(1, 2, 0, 3).reshape(tokens, D)
    mixed = (conv + skip_bias[None, :] * gated.astype(jnp.float32)).astype(jnp.bfloat16)
    return (post_gate.astype(jnp.float32) * mixed.astype(jnp.float32)).astype(jnp.bfloat16)
```

```python
import functools
import math

import jax
import jax.numpy as jnp
from jax import lax
from jax.experimental import pallas as pl
from jax.experimental.pallas import tpu as pltpu
from jax.sharding import PartitionSpec as P

BLK = 128
TILE_BLOCKS = 8
MESH = pl.DeviceIdType.MESH


def kernel(
    stretch, ctx, chunks, lags, width,
    pre_ref, val_ref, post_ref, filt_ref, skip_ref, live_ref, out_ref,
    gated, arrived, mixed, back, toeplitz,
    send_in, recv_in, send_back, recv_back,
):
    n = stretch * ctx
    me = lax.axis_index("stretch") * ctx + lax.axis_index("ctx")
    rows = gated.shape[2]
    share = chunks * rows
    chunk_groups = rows // width
    stride = 5 if math.gcd(5, n) == 1 else 1

    def peer(k):
        return lax.rem(me + k * stride, n)

    def place(device):
        return (device // ctx, lax.rem(device, ctx))

    def slab_of(device):
        return lax.rem(device, ctx) * stretch + device // ctx

    barrier = pltpu.get_barrier_semaphore()

    @pl.loop(1, n)
    def _(k):
        pl.semaphore_signal(barrier, inc=1, device_id=place(peer(k)), device_id_type=MESH)

    unit = max(share, BLK)

    @pl.loop(0, n * share // unit)
    def _(tile):
        lanes = pl.ds(pl.multiple_of(tile * unit, unit), unit)
        product = pre_ref[:, lanes].astype(jnp.float32) * val_ref[:, lanes].astype(jnp.float32)
        turned = product.T.astype(jnp.bfloat16)
        for device in range(unit // share):
            for chunk in range(chunks):
                first = device * share + chunk * rows
                gated[chunk, tile * (unit // share) + device] = turned[first : first + rows]

    pl.semaphore_wait(barrier, n - 1)

    def copy_in(chunk, device, slot):
        return pltpu.make_async_remote_copy(
            src_ref=gated.at[chunk, slab_of(device)],
            dst_ref=arrived.at[chunk, slot],
            send_sem=send_in.at[chunk, device],
            recv_sem=recv_in.at[chunk, slot],
            device_id=place(device),
            device_id_type=MESH,
        )

    def copy_back(chunk, device, slot):
        return pltpu.make_async_remote_copy(
            src_ref=mixed.at[chunk, device],
            dst_ref=back.at[chunk, slot],
            send_sem=send_back.at[chunk, device],
            recv_sem=recv_back.at[chunk, slot],
            device_id=place(device),
            device_id_type=MESH,
        )

    for chunk in range(chunks):

        @pl.loop(1, n)
        def _(k, chunk=chunk):
            copy_in(chunk, peer(k), me).start()

    for chunk in range(chunks):
        arrived[chunk, me] = gated[chunk, slab_of(me)]

    @pl.loop(0, chunks * chunk_groups)
    def _(group):
        for lag in range(lags):
            taps = filt_ref[pl.ds(group, 1), lag * BLK : (lag + 2) * BLK]
            spread = jnp.broadcast_to(taps, (BLK, 2 * BLK))
            turned = pltpu.roll(spread, 0, 1, stride=1, stride_axis=0)
            toeplitz[group, lag * BLK : (lag + 1) * BLK, :] = turned[:, BLK:].astype(jnp.bfloat16)

    for chunk in range(chunks):

        @pl.loop(1, n)
        def _(k, chunk=chunk):
            copy_in(chunk, me, peer(k)).wait_recv()

        @pl.loop(0, chunk_groups * (n // TILE_BLOCKS))
        def _(step, chunk=chunk):
            group = step // (n // TILE_BLOCKS)
            first = lax.rem(step, n // TILE_BLOCKS) * TILE_BLOCKS
            channels = pl.ds(pl.multiple_of(group * width, width), width)
            columns = []
            for lag in range(lags):
                pieces = []
                for block in range(TILE_BLOCKS):
                    source = lax.rem(first + (block - lag + n), n)
                    live = live_ref[first + block, lag]
                    live = jnp.concatenate([live] * (width // live.shape[0]), axis=0)
                    pieces.append(arrived[chunk, source, channels, :] * live)
                columns.append(jnp.concatenate(pieces, axis=0))
            window = jnp.concatenate(columns, axis=1)
            conv = jnp.dot(
                window, toeplitz[chunk * chunk_groups + group], preferred_element_type=jnp.float32
            )
            skip = skip_ref[pl.ds(pl.multiple_of(chunk * rows + group * width, width), width), :]
            for block in range(TILE_BLOCKS):
                direct = arrived[chunk, first + block, channels, :].astype(jnp.float32)
                total = conv[block * width : (block + 1) * width] + skip * direct
                mixed[chunk, first + block, channels, :] = total.astype(jnp.bfloat16)

        @pl.loop(1, n)
        def _(k, chunk=chunk):
            copy_back(chunk, peer(k), me).start()

        back[chunk, me] = mixed[chunk, me]

    def finish(lanes, turned):
        product = turned.astype(jnp.float32).T * post_ref[:, lanes].astype(jnp.float32)
        out_ref[:, lanes] = product.astype(jnp.bfloat16)

    for chunk in range(chunks):

        @pl.loop(0, n)
        def _(k, chunk=chunk):
            device = peer(k)

            @pl.when(k > 0)
            def _():
                copy_back(chunk, me, device).wait_recv()

            if rows % BLK == 0:
                lanes = pl.ds(pl.multiple_of(slab_of(device) * share + chunk * rows, BLK), rows)
                finish(lanes, back[chunk, device])

    if rows % BLK != 0:
        per = BLK // rows

        @pl.loop(0, n // per)
        def _(tile):
            slabs = [tile * per + index for index in range(per)]
            pieces = [back[0, lax.rem(slab, stretch) * ctx + slab // stretch] for slab in slabs]
            turned = jnp.concatenate(pieces, axis=0)
            finish(pl.ds(pl.multiple_of(tile * BLK, BLK), BLK), turned)

    for chunk in range(chunks):

        @pl.loop(1, n)
        def _(k, chunk=chunk):
            copy_in(chunk, peer(k), me).wait_send()
            copy_back(chunk, peer(k), me).wait_send()


def per_device(stretch, ctx, post_gate, pre_gate, values, filters, skip_bias, doc_blocks):
    n = stretch * ctx
    tok_rows, model = values.shape
    taps = filters.shape[1]
    share = model // n
    groups = filters.shape[0] // stretch
    width = share // groups
    blocks = n * tok_rows // BLK
    longest = blocks * 3 // 8
    lags = min(longest, taps // BLK + 1)
    chunks = share // BLK if share % BLK == 0 else 1
    rows = share // chunks
    part = lax.axis_index("stretch")
    own_filters = lax.dynamic_slice_in_dim(filters, part * groups, groups, 0)
    own_filters = jnp.pad(own_filters, ((0, 0), (BLK, BLK)))
    own_skip = lax.dynamic_slice_in_dim(skip_bias, part * share, share, 0)
    own_skip = jnp.broadcast_to(own_skip[:, None], (share, BLK))
    ids = jnp.arange(blocks, dtype=jnp.int32)
    ends = jnp.cumsum(doc_blocks)
    starts = jnp.max(jnp.where(ends[None, :] <= ids[:, None], ends[None, :], 0), axis=1)
    live = (ids[:, None] - jnp.arange(lags, dtype=jnp.int32)[None, :]) >= starts[:, None]
    live = jnp.broadcast_to(live.astype(jnp.bfloat16)[:, :, None, None], (blocks, lags, 16, BLK))
    slab = (chunks, n, rows, BLK)
    vmem = pl.BlockSpec(memory_space=pltpu.VMEM)
    sems = pltpu.SemaphoreType.DMA((chunks, n))
    return pl.pallas_call(
        functools.partial(kernel, stretch, ctx, chunks, lags, width),
        out_shape=jax.ShapeDtypeStruct((tok_rows, model), jnp.bfloat16),
        in_specs=[vmem] * 6,
        out_specs=vmem,
        scratch_shapes=[
            pltpu.VMEM(slab, jnp.bfloat16),
            pltpu.VMEM(slab, jnp.bfloat16),
            pltpu.VMEM(slab, jnp.bfloat16),
            pltpu.VMEM(slab, jnp.bfloat16),
            pltpu.VMEM((groups, lags * BLK, BLK), jnp.bfloat16),
            sems, sems, sems, sems,
        ],
        compiler_params=pltpu.CompilerParams(
            collective_id=0, has_side_effects=True, vmem_limit_bytes=56 * 1024 * 1024
        ),
    )(pre_gate, values, post_gate, own_filters, own_skip, live)


def solution(mesh):
    rows = P(("stretch", "ctx"), None)
    body = functools.partial(per_device, mesh.shape["stretch"], mesh.shape["ctx"])
    return jax.shard_map(
        body,
        mesh=mesh,
        in_specs=(rows, rows, rows, P("ctx", None), P("ctx"), P()),
        out_specs=rows,
        check_vma=False,
    )
```

```python
import functools
import math

import jax
import jax.numpy as jnp
from jax import lax
from jax.experimental import pallas as pl
from jax.experimental.pallas import tpu as pltpu
from jax.sharding import PartitionSpec as P

BLK = 128
TILE_BLOCKS = 8
MESH = pl.DeviceIdType.MESH


def kernel(
    stretch, ctx, chunks, lags, width,
    pre_ref, val_ref, filt_ref, skip_ref, docs_ref, out_ref,
    pre, val, gated, arrived, mixed, back, toeplitz, skips, live,
    load_sem, send_in, recv_in, send_back, recv_back,
):
    loads = [
        pltpu.make_async_copy(pre_ref, pre, load_sem.at[0]),
        pltpu.make_async_copy(val_ref, val, load_sem.at[1]),
    ]
    for load in loads:
        load.start()
    part = lax.axis_index("stretch")
    n = stretch * ctx
    me = lax.axis_index("stretch") * ctx + lax.axis_index("ctx")
    rows = gated.shape[2]
    share = chunks * rows
    chunk_groups = rows // width
    stride = 5 if math.gcd(5, n) == 1 else 1

    def peer(k):
        return lax.rem(me + k * stride, n)

    def place(device):
        return (device // ctx, lax.rem(device, ctx))

    def slab_of(device):
        return lax.rem(device, ctx) * stretch + device // ctx

    barrier = pltpu.get_barrier_semaphore()

    @pl.loop(1, n)
    def _(k):
        pl.semaphore_signal(barrier, inc=1, device_id=place(peer(k)), device_id_type=MESH)

    def copy_in(chunk, device, slot):
        return pltpu.make_async_remote_copy(
            src_ref=gated.at[chunk, slab_of(device)],
            dst_ref=arrived.at[chunk, slot],
            send_sem=send_in.at[chunk, device],
            recv_sem=recv_in.at[chunk, slot],
            device_id=place(device),
            device_id_type=MESH,
        )

    def copy_back(chunk, device, slot):
        return pltpu.make_async_remote_copy(
            src_ref=mixed.at[chunk, device],
            dst_ref=back.at[chunk, slot],
            send_sem=send_back.at[chunk, device],
            recv_sem=recv_back.at[chunk, slot],
            device_id=place(device),
            device_id_type=MESH,
        )

    unit = max(share, BLK)
    per_unit = unit // share

    def gate(tile):
        lanes = pl.ds(pl.multiple_of(tile * unit, unit), unit)
        product = pre[:, lanes].astype(jnp.float32) * val[:, lanes].astype(jnp.float32)
        turned = product.T.astype(jnp.bfloat16)
        for slab in range(per_unit):
            for chunk in range(chunks):
                first = slab * share + chunk * rows
                gated[chunk, tile * per_unit + slab] = turned[first : first + rows]

    for load in loads:
        load.wait()
    early = n // 4 if per_unit == 1 else n

    if per_unit == 1:

        @pl.loop(0, early)
        def _(k):
            gate(slab_of(peer(k)))

    else:

        @pl.loop(0, n // per_unit)
        def _(tile):
            gate(tile)

    pl.semaphore_wait(barrier, n - 1)

    @pl.loop(1, early)
    def _(k):
        copy_in(0, peer(k), me).start()

    @pl.loop(early, n)
    def _(k):
        gate(slab_of(peer(k)))
        copy_in(0, peer(k), me).start()

    for chunk in range(chunks):
        arrived[chunk, me] = gated[chunk, slab_of(me)]

    taps = filt_ref.shape[1]

    @pl.loop(0, chunks * chunk_groups)
    def _(group):
        row = part * (chunks * chunk_groups) + group
        chosen = lax.broadcasted_iota(jnp.int32, (filt_ref.shape[0], BLK), 0) == row
        for lag in range(lags):
            pieces = []
            for first in ((lag - 1) * BLK, lag * BLK):
                if 0 <= first < taps:
                    picked = jnp.where(chosen, filt_ref[:, first : first + BLK], 0.0)
                    pieces.append(jnp.sum(picked, axis=0, keepdims=True))
                else:
                    pieces.append(jnp.zeros((1, BLK), jnp.float32))
            spread = jnp.broadcast_to(jnp.concatenate(pieces, axis=1), (BLK, 2 * BLK))
            turned = pltpu.roll(spread, 0, 1, stride=1, stride_axis=0)
            toeplitz[group, lag * BLK : (lag + 1) * BLK, :] = turned[:, BLK:].astype(jnp.bfloat16)

    skips[...] = jnp.broadcast_to(skip_ref[pl.ds(part, 1), :], (BLK, share)).T
    ends = []
    for doc in range(docs_ref.shape[0]):
        ends.append(docs_ref[doc] + (ends[-1] if ends else 0))

    @pl.loop(0, n)
    def _(block):
        start = jnp.int32(0)
        for end in ends:
            start = jnp.maximum(start, jnp.where(end <= block, end, 0))
        for lag in range(lags):
            weight = jnp.where(block - lag >= start, 1.0, 0.0).astype(jnp.float32)
            live[block, lag] = jnp.full(live.shape[2:], weight, jnp.float32).astype(jnp.bfloat16)

    for chunk in range(1, chunks):

        @pl.loop(1, n)
        def _(k, chunk=chunk):
            copy_in(chunk - 1, peer(k), me).wait_send()
            copy_in(chunk, peer(k), me).start()

    for chunk in range(chunks):

        @pl.loop(1, n)
        def _(k, chunk=chunk):
            copy_in(chunk, me, peer(k)).wait_recv()

        @pl.loop(0, chunk_groups * (n // TILE_BLOCKS))
        def _(step, chunk=chunk):
            group = step // (n // TILE_BLOCKS)
            first = lax.rem(step, n // TILE_BLOCKS) * TILE_BLOCKS
            channels = pl.ds(pl.multiple_of(group * width, width), width)
            columns = []
            for lag in range(lags):
                pieces = []
                for block in range(TILE_BLOCKS):
                    source = lax.rem(first + (block - lag + n), n)
                    kept = jnp.concatenate([live[first + block, lag]] * (width // live.shape[2]), axis=0)
                    pieces.append(arrived[chunk, source, channels, :] * kept)
                columns.append(jnp.concatenate(pieces, axis=0))
            window = jnp.concatenate(columns, axis=1)
            conv = jnp.dot(
                window, toeplitz[chunk * chunk_groups + group], preferred_element_type=jnp.float32
            )
            skip = skips[pl.ds(pl.multiple_of(chunk * rows + group * width, width), width), :]
            for block in range(TILE_BLOCKS):
                direct = arrived[chunk, first + block, channels, :].astype(jnp.float32)
                total = conv[block * width : (block + 1) * width] + skip * direct
                mixed[chunk, first + block, channels, :] = total.astype(jnp.bfloat16)

        @pl.loop(1, n)
        def _(k, chunk=chunk):
            if chunk == 0:
                copy_in(chunks - 1, peer(k), me).wait_send()
            copy_back(chunk, peer(k), me).start()

        back[chunk, me] = mixed[chunk, me]

    def finish(lanes, turned):
        out_ref[:, lanes] = turned.astype(jnp.float32).T.astype(jnp.bfloat16)

    for chunk in range(chunks):

        @pl.loop(0, n)
        def _(k, chunk=chunk):
            device = peer(k)

            @pl.when(k > 0)
            def _():
                copy_back(chunk, me, device).wait_recv()

            if rows % BLK == 0:
                lanes = pl.ds(pl.multiple_of(slab_of(device) * share + chunk * rows, BLK), rows)
                finish(lanes, back[chunk, device])

    if rows % BLK != 0:
        per = BLK // rows

        @pl.loop(0, n // per)
        def _(tile):
            slabs = [tile * per + index for index in range(per)]
            pieces = [back[0, lax.rem(slab, stretch) * ctx + slab // stretch] for slab in slabs]
            turned = jnp.concatenate(pieces, axis=0)
            finish(pl.ds(pl.multiple_of(tile * BLK, BLK), BLK), turned)

    for chunk in range(chunks):

        @pl.loop(1, n)
        def _(k, chunk=chunk):
            copy_back(chunk, peer(k), me).wait_send()


def per_device(stretch, ctx, post_gate, pre_gate, values, filters, skip_bias, doc_blocks):
    n = stretch * ctx
    tok_rows, model = values.shape
    taps = filters.shape[1]
    share = model // n
    groups = filters.shape[0] // stretch
    width = share // groups
    blocks = n * tok_rows // BLK
    longest = blocks * 3 // 8
    lags = min(longest, taps // BLK + 1)
    chunks = share // BLK if share % BLK == 0 else 1
    rows = share // chunks
    slab = (chunks, n, rows, BLK)
    vmem = pl.BlockSpec(memory_space=pltpu.VMEM)
    sems = pltpu.SemaphoreType.DMA((chunks, n))
    returned = pl.pallas_call(
        functools.partial(kernel, stretch, ctx, chunks, lags, width),
        out_shape=jax.ShapeDtypeStruct((tok_rows, model), jnp.bfloat16),
        in_specs=[
            pl.BlockSpec(memory_space=pltpu.HBM),
            pl.BlockSpec(memory_space=pltpu.HBM),
            vmem,
            vmem,
            pl.BlockSpec(memory_space=pltpu.SMEM),
        ],
        out_specs=vmem,
        scratch_shapes=[
            pltpu.VMEM((tok_rows, model), jnp.bfloat16),
            pltpu.VMEM((tok_rows, model), jnp.bfloat16),
            pltpu.VMEM(slab, jnp.bfloat16),
            pltpu.VMEM(slab, jnp.bfloat16),
            pltpu.VMEM(slab, jnp.bfloat16),
            pltpu.VMEM(slab, jnp.bfloat16),
            pltpu.VMEM((groups, lags * BLK, BLK), jnp.bfloat16),
            pltpu.VMEM((share, BLK), jnp.float32),
            pltpu.VMEM((blocks, lags, 16, BLK), jnp.bfloat16),
            pltpu.SemaphoreType.DMA((2,)),
            sems, sems, sems, sems,
        ],
        compiler_params=pltpu.CompilerParams(
            collective_id=0, has_side_effects=True, vmem_limit_bytes=44 * 1024 * 1024
        ),
    )(pre_gate, values, filters, skip_bias.reshape(stretch, share), doc_blocks)
    return (post_gate.astype(jnp.float32) * returned.astype(jnp.float32)).astype(jnp.bfloat16)


def solution(mesh):
    rows = P(("stretch", "ctx"), None)
    body = functools.partial(per_device, mesh.shape["stretch"], mesh.shape["ctx"])
    return jax.shard_map(
        body,
        mesh=mesh,
        in_specs=(rows, rows, rows, P("ctx", None), P("ctx"), P()),
        out_specs=rows,
        check_vma=False,
    )
```

```python
import functools

import jax
import jax.numpy as jnp
from jax import lax
from jax.experimental import pallas as pl
from jax.experimental.pallas import tpu as pltpu
from jax.sharding import PartitionSpec as P

BLK = 128
TILE_BLOCKS = 8
MESH = pl.DeviceIdType.MESH


def kernel(
    stretch, ctx, chunks, lags, width,
    pre_ref, val_ref, filt_ref, skip_ref, docs_ref, out_ref,
    pre, val, filt, gated, arrived, mixed, back, toeplitz, skips, live,
    load_sem, send_in, recv_in, send_back, recv_back,
):
    loads = [
        pltpu.make_async_copy(pre_ref, pre, load_sem.at[0]),
        pltpu.make_async_copy(val_ref, val, load_sem.at[1]),
        pltpu.make_async_copy(filt_ref, filt, load_sem.at[2]),
    ]
    for load in loads:
        load.start()
    part = lax.axis_index("stretch")
    n = stretch * ctx
    me = lax.axis_index("stretch") * ctx + lax.axis_index("ctx")
    rows = gated.shape[2]
    share = chunks * rows
    chunk_groups = rows // width
    halves = 2 if ctx % 2 == 0 else 1
    half = ctx // halves
    my_part, my_place = lax.axis_index("stretch"), lax.axis_index("ctx")

    def peer(k):
        step = k // halves
        column = lax.rem(my_part + lax.rem(step, stretch), stretch)
        side = lax.rem(my_place // half + lax.rem(k, halves), halves)
        return column * ctx + side * half + lax.rem(lax.rem(my_place, half) + step // stretch, half)

    def place(device):
        return (device // ctx, lax.rem(device, ctx))

    def slab_of(device):
        return lax.rem(device, ctx) * stretch + device // ctx

    barrier = pltpu.get_barrier_semaphore()

    @pl.loop(1, n)
    def _(k):
        pl.semaphore_signal(barrier, inc=1, device_id=place(peer(k)), device_id_type=MESH)

    def copy_in(chunk, device, slot):
        return pltpu.make_async_remote_copy(
            src_ref=gated.at[chunk, slab_of(device)],
            dst_ref=arrived.at[chunk, slot],
            send_sem=send_in.at[chunk, device],
            recv_sem=recv_in.at[chunk, slot],
            device_id=place(device),
            device_id_type=MESH,
        )

    def copy_back(chunk, device, slot):
        return pltpu.make_async_remote_copy(
            src_ref=mixed.at[chunk, device],
            dst_ref=back.at[chunk, slot],
            send_sem=send_back.at[chunk, device],
            recv_sem=recv_back.at[chunk, slot],
            device_id=place(device),
            device_id_type=MESH,
        )

    unit = max(share, BLK)
    per_unit = unit // share

    def gate(tile):
        lanes = pl.ds(pl.multiple_of(tile * unit, unit), unit)
        product = pre[:, lanes].astype(jnp.float32) * val[:, lanes].astype(jnp.float32)
        turned = product.T.astype(jnp.bfloat16)
        for slab in range(per_unit):
            for chunk in range(chunks):
                first = slab * share + chunk * rows
                gated[chunk, tile * per_unit + slab] = turned[first : first + rows]

    for load in loads[:2]:
        load.wait()
    early = n // 4 if per_unit == 1 else n

    if per_unit == 1:

        @pl.loop(0, early)
        def _(k):
            gate(slab_of(peer(k)))

    else:

        @pl.loop(0, n // per_unit)
        def _(tile):
            gate(tile)

    pl.semaphore_wait(barrier, n - 1)

    @pl.loop(1, early)
    def _(k):
        copy_in(0, peer(k), me).start()

    @pl.loop(early, n)
    def _(k):
        gate(slab_of(peer(k)))
        copy_in(0, peer(k), me).start()

    for chunk in range(chunks):
        arrived[chunk, me] = gated[chunk, slab_of(me)]

    loads[2].wait()
    taps = filt.shape[1]

    @pl.loop(0, chunks * chunk_groups)
    def _(group):
        row = part * (chunks * chunk_groups) + group
        chosen = lax.broadcasted_iota(jnp.int32, (filt.shape[0], BLK), 0) == row
        for lag in range(lags):
            pieces = []
            for first in ((lag - 1) * BLK, lag * BLK):
                if 0 <= first < taps:
                    picked = jnp.where(chosen, filt[:, first : first + BLK], 0.0)
                    pieces.append(jnp.sum(picked, axis=0, keepdims=True))
                else:
                    pieces.append(jnp.zeros((1, BLK), jnp.float32))
            spread = jnp.broadcast_to(jnp.concatenate(pieces, axis=1), (BLK, 2 * BLK))
            turned = pltpu.roll(spread, 0, 1, stride=1, stride_axis=0)
            toeplitz[group, lag * BLK : (lag + 1) * BLK, :] = turned[:, BLK:].astype(jnp.bfloat16)

    skips[...] = jnp.broadcast_to(skip_ref[...].reshape(1, stretch * share), (BLK, stretch * share)).T
    ends = []
    for doc in range(docs_ref.shape[0]):
        ends.append(docs_ref[doc] + (ends[-1] if ends else 0))

    @pl.loop(0, n)
    def _(block):
        start = jnp.int32(0)
        for end in ends:
            start = jnp.maximum(start, jnp.where(end <= block, end, 0))
        for lag in range(lags):
            weight = jnp.where(block - lag >= start, 1.0, 0.0).astype(jnp.float32)
            live[block, lag] = jnp.full(live.shape[2:], weight, jnp.float32).astype(jnp.bfloat16)

    if chunks > 1:

        @pl.loop(1, n)
        def _(k):
            copy_in(1, peer(k), me).start()

    for chunk in range(chunks):

        @pl.loop(1, n)
        def _(k, chunk=chunk):
            if chunk + 2 < chunks:
                copy_in(chunk, peer(k), me).wait_send()
                copy_in(chunk + 2, peer(k), me).start()

        @pl.loop(1, n)
        def _(k, chunk=chunk):
            copy_in(chunk, me, peer(k)).wait_recv()

        @pl.loop(0, chunk_groups * (n // TILE_BLOCKS))
        def _(step, chunk=chunk):
            group = step // (n // TILE_BLOCKS)
            first = lax.rem(step, n // TILE_BLOCKS) * TILE_BLOCKS
            channels = pl.ds(pl.multiple_of(group * width, width), width)
            columns = []
            for lag in range(lags):
                pieces = []
                for block in range(TILE_BLOCKS):
                    source = lax.rem(first + (block - lag + n), n)
                    kept = jnp.concatenate([live[first + block, lag]] * (width // live.shape[2]), axis=0)
                    pieces.append(arrived[chunk, source, channels, :] * kept)
                columns.append(jnp.concatenate(pieces, axis=0))
            window = jnp.concatenate(columns, axis=1)
            conv = jnp.dot(
                window, toeplitz[chunk * chunk_groups + group], preferred_element_type=jnp.float32
            )
            skip_row = part * share + chunk * rows + group * width
            skip = skips[pl.ds(pl.multiple_of(skip_row, width), width), :]
            for block in range(TILE_BLOCKS):
                direct = arrived[chunk, first + block, channels, :].astype(jnp.float32)
                total = conv[block * width : (block + 1) * width] + skip * direct
                mixed[chunk, first + block, channels, :] = total.astype(jnp.bfloat16)

        back[chunk, me] = mixed[chunk, me]

        if chunk == chunks - 2:
            ready = range(chunks - 1)
        else:
            ready = [chunk] if chunk == chunks - 1 else []
        for done in ready:

            @pl.loop(1, n)
            def _(k, done=done):
                copy_back(done, peer(k), me).start()

    def finish(lanes, turned):
        out_ref[:, lanes] = turned.astype(jnp.float32).T.astype(jnp.bfloat16)

    joint = max(BLK // rows, 1)
    if share % BLK == 0:
        for first in range(0, chunks, joint):

            @pl.loop(0, n)
            def _(k, first=first):
                device = peer(k)

                @pl.when(k > 0)
                def _():
                    for chunk in range(first, first + joint):
                        copy_back(chunk, me, device).wait_recv()

                pieces = [back[chunk, device] for chunk in range(first, first + joint)]
                lane = slab_of(device) * share + first * rows
                finish(pl.ds(pl.multiple_of(lane, BLK), joint * rows), jnp.concatenate(pieces, axis=0))

    else:

        @pl.loop(1, n)
        def _(k):
            copy_back(0, me, peer(k)).wait_recv()

        @pl.loop(0, n // joint)
        def _(tile):
            slabs = [tile * joint + index for index in range(joint)]
            pieces = [back[0, lax.rem(slab, stretch) * ctx + slab // stretch] for slab in slabs]
            finish(pl.ds(pl.multiple_of(tile * BLK, BLK), BLK), jnp.concatenate(pieces, axis=0))

    for chunk in range(chunks):

        @pl.loop(1, n)
        def _(k, chunk=chunk):
            if chunk + 2 >= chunks:
                copy_in(chunk, peer(k), me).wait_send()
            copy_back(chunk, peer(k), me).wait_send()


def per_device(stretch, ctx, post_gate, pre_gate, values, filters, skip_bias, doc_blocks):
    n = stretch * ctx
    tok_rows, model = values.shape
    taps = filters.shape[1]
    share = model // n
    groups = filters.shape[0] // stretch
    width = share // groups
    blocks = n * tok_rows // BLK
    longest = blocks * 3 // 8
    lags = min(longest, taps // BLK + 1)
    chunks = share // (2 * width) if share % BLK == 0 else 1
    rows = share // chunks
    slab = (chunks, n, rows, BLK)
    vmem = pl.BlockSpec(memory_space=pltpu.VMEM)
    sems = pltpu.SemaphoreType.DMA((chunks, n))
    returned = pl.pallas_call(
        functools.partial(kernel, stretch, ctx, chunks, lags, width),
        out_shape=jax.ShapeDtypeStruct((tok_rows, model), jnp.bfloat16),
        in_specs=[
            pl.BlockSpec(memory_space=pltpu.HBM),
            pl.BlockSpec(memory_space=pltpu.HBM),
            pl.BlockSpec(memory_space=pltpu.HBM),
            vmem,
            pl.BlockSpec(memory_space=pltpu.SMEM),
        ],
        out_specs=vmem,
        scratch_shapes=[
            pltpu.VMEM((tok_rows, model), jnp.bfloat16),
            pltpu.VMEM((tok_rows, model), jnp.bfloat16),
            pltpu.VMEM(filters.shape, jnp.float32),
            pltpu.VMEM(slab, jnp.bfloat16),
            pltpu.VMEM(slab, jnp.bfloat16),
            pltpu.VMEM(slab, jnp.bfloat16),
            pltpu.VMEM(slab, jnp.bfloat16),
            pltpu.VMEM((groups, lags * BLK, BLK), jnp.bfloat16),
            pltpu.VMEM((stretch * share, BLK), jnp.float32),
            pltpu.VMEM((blocks, lags, 16, BLK), jnp.bfloat16),
            pltpu.SemaphoreType.DMA((3,)),
            sems, sems, sems, sems,
        ],
        compiler_params=pltpu.CompilerParams(
            collective_id=0, has_side_effects=True, vmem_limit_bytes=62 * 1024 * 1024
        ),
    )(pre_gate, values, filters, skip_bias, doc_blocks)
    return (post_gate.astype(jnp.float32) * returned.astype(jnp.float32)).astype(jnp.bfloat16)


def solution(mesh):
    rows = P(("stretch", "ctx"), None)
    body = functools.partial(per_device, mesh.shape["stretch"], mesh.shape["ctx"])
    return jax.shard_map(
        body,
        mesh=mesh,
        in_specs=(rows, rows, rows, P("ctx", None), P("ctx"), P()),
        out_specs=rows,
        check_vma=False,
    )
```

```python
import functools

import jax
import jax.numpy as jnp
from jax import lax
from jax.experimental import pallas as pl
from jax.experimental.pallas import tpu as pltpu
from jax.sharding import PartitionSpec as P

BLK = 128
TILE_BLOCKS = 8
MESH = pl.DeviceIdType.MESH


def kernel(
    stretch, ctx, chunks, lags, width,
    pre_ref, val_ref, filt_ref, skip_ref, docs_ref, out_ref,
    pre, val, filt, gated, arrived, mixed, back, toeplitz, skips, live,
    load_sem, send_in, recv_in, send_back, recv_back,
):
    loads = [
        pltpu.make_async_copy(pre_ref, pre, load_sem.at[0]),
        pltpu.make_async_copy(val_ref, val, load_sem.at[1]),
        pltpu.make_async_copy(filt_ref, filt, load_sem.at[2]),
    ]
    for load in loads:
        load.start()
    part = lax.axis_index("stretch")
    n = stretch * ctx
    me = lax.axis_index("stretch") * ctx + lax.axis_index("ctx")
    rows = gated.shape[2]
    share = chunks * rows
    lead = lags - 1
    chunk_groups = rows // width
    halves = 2 if ctx % 2 == 0 else 1
    half = ctx // halves
    my_part, my_place = lax.axis_index("stretch"), lax.axis_index("ctx")

    def peer(k):
        step = k // halves
        column = lax.rem(my_part + lax.rem(step, stretch), stretch)
        side = lax.rem(my_place // half + lax.rem(k, halves), halves)
        return column * ctx + side * half + lax.rem(lax.rem(my_place, half) + step // stretch, half)

    def place(device):
        return (device // ctx, lax.rem(device, ctx))

    def slab_of(device):
        return lax.rem(device, ctx) * stretch + device // ctx

    barrier = pltpu.get_barrier_semaphore()

    @pl.loop(1, n)
    def _(k):
        pl.semaphore_signal(barrier, inc=1, device_id=place(peer(k)), device_id_type=MESH)

    def copy_in(chunk, device, slot):
        return pltpu.make_async_remote_copy(
            src_ref=gated.at[chunk, slab_of(device)],
            dst_ref=arrived.at[chunk, lead + slot],
            send_sem=send_in.at[chunk, device],
            recv_sem=recv_in.at[chunk, slot],
            device_id=place(device),
            device_id_type=MESH,
        )

    def copy_back(chunk, device, slot):
        return pltpu.make_async_remote_copy(
            src_ref=mixed.at[chunk, device],
            dst_ref=back.at[chunk, slot],
            send_sem=send_back.at[chunk, device],
            recv_sem=recv_back.at[chunk, slot],
            device_id=place(device),
            device_id_type=MESH,
        )

    unit = max(share, BLK)
    per_unit = unit // share

    def gate(tile):
        lanes = pl.ds(pl.multiple_of(tile * unit, unit), unit)
        product = pre[:, lanes].astype(jnp.float32) * val[:, lanes].astype(jnp.float32)
        turned = product.T.astype(jnp.bfloat16)
        for slab in range(per_unit):
            for chunk in range(chunks):
                first = slab * share + chunk * rows
                gated[chunk, tile * per_unit + slab] = turned[first : first + rows]

    for load in loads[:2]:
        load.wait()
    early = n // 4 if per_unit == 1 else n

    if per_unit == 1:

        @pl.loop(0, early)
        def _(k):
            gate(slab_of(peer(k)))

    else:

        @pl.loop(0, n // per_unit)
        def _(tile):
            gate(tile)

    pl.semaphore_wait(barrier, n - 1)

    @pl.loop(1, early)
    def _(k):
        copy_in(0, peer(k), me).start()

    @pl.loop(early, n)
    def _(k):
        gate(slab_of(peer(k)))
        copy_in(0, peer(k), me).start()

    for chunk in range(chunks):
        arrived[chunk, lead + me] = gated[chunk, slab_of(me)]
        arrived[chunk, 0:lead] = jnp.zeros((lead, rows, BLK), jnp.bfloat16)

    loads[2].wait()
    taps = filt.shape[1]

    @pl.loop(0, chunks * chunk_groups)
    def _(group):
        row = part * (chunks * chunk_groups) + group
        chosen = lax.broadcasted_iota(jnp.int32, (filt.shape[0], BLK), 0) == row
        for lag in range(lags):
            pieces = []
            for first in ((lag - 1) * BLK, lag * BLK):
                if 0 <= first < taps:
                    picked = jnp.where(chosen, filt[:, first : first + BLK], 0.0)
                    pieces.append(jnp.sum(picked, axis=0, keepdims=True))
                else:
                    pieces.append(jnp.zeros((1, BLK), jnp.float32))
            spread = jnp.broadcast_to(jnp.concatenate(pieces, axis=1), (BLK, 2 * BLK))
            turned = pltpu.roll(spread, 0, 1, stride=1, stride_axis=0)
            toeplitz[group, lag * BLK : (lag + 1) * BLK, :] = turned[:, BLK:].astype(jnp.bfloat16)

    skips[...] = jnp.broadcast_to(skip_ref[...].reshape(1, stretch * share), (BLK, stretch * share)).T
    ends = []
    for doc in range(docs_ref.shape[0]):
        ends.append(docs_ref[doc] + (ends[-1] if ends else 0))

    @pl.loop(0, n)
    def _(block):
        start = jnp.int32(0)
        for end in ends:
            start = jnp.maximum(start, jnp.where(end <= block, end, 0))
        for lag in range(lags):
            weight = jnp.where(block - lag >= start, 1.0, 0.0).astype(jnp.float32)
            live[block, lag] = jnp.full(live.shape[2:], weight, jnp.float32).astype(jnp.bfloat16)

    if chunks > 1:

        @pl.loop(1, n)
        def _(k):
            copy_in(1, peer(k), me).start()

    for chunk in range(chunks):

        @pl.loop(1, n)
        def _(k, chunk=chunk):
            if chunk == 0 and chunks > 2:
                copy_in(0, peer(k), me).wait_send()
                copy_in(2, peer(k), me).start()

        @pl.loop(1, n)
        def _(k, chunk=chunk):
            copy_in(chunk, me, peer(k)).wait_recv()

        @pl.loop(0, chunk_groups * (n // TILE_BLOCKS))
        def _(step, chunk=chunk):
            group = step // (n // TILE_BLOCKS)
            first = lax.rem(step, n // TILE_BLOCKS) * TILE_BLOCKS
            channels = pl.ds(pl.multiple_of(group * width, width), width)
            columns = []
            for lag in range(lags):
                pieces = []
                for block in range(TILE_BLOCKS):
                    source = first + (lead + block - lag)
                    kept = jnp.concatenate([live[first + block, lag]] * (width // live.shape[2]), axis=0)
                    pieces.append(arrived[chunk, source, channels, :] * kept)
                columns.append(jnp.concatenate(pieces, axis=0))
            window = jnp.concatenate(columns, axis=1)
            conv = jnp.dot(
                window, toeplitz[chunk * chunk_groups + group], preferred_element_type=jnp.float32
            )
            skip_row = part * share + chunk * rows + group * width
            skip = skips[pl.ds(pl.multiple_of(skip_row, width), width), :]
            for block in range(TILE_BLOCKS):
                direct = arrived[chunk, first + (lead + block), channels, :].astype(jnp.float32)
                total = conv[block * width : (block + 1) * width] + skip * direct
                mixed[chunk, first + block, channels, :] = total.astype(jnp.bfloat16)

        back[chunk, me] = mixed[chunk, me]

        for later in range(3, chunks) if chunk == 0 else ():

            @pl.loop(1, n)
            def _(k, later=later):
                copy_in(later - 2, peer(k), me).wait_send()
                copy_in(later, peer(k), me).start()

        @pl.loop(1, n)
        def _(k, chunk=chunk):
            copy_back(chunk, peer(k), me).start()

    def finish(lanes, turned):
        out_ref[:, lanes] = turned.astype(jnp.float32).T.astype(jnp.bfloat16)

    joint = max(BLK // rows, 1)
    if share % BLK == 0:
        for first in range(0, chunks, joint):

            @pl.loop(0, n)
            def _(k, first=first):
                device = peer(k)

                @pl.when(k > 0)
                def _():
                    for chunk in range(first, first + joint):
                        copy_back(chunk, me, device).wait_recv()

                pieces = [back[chunk, device] for chunk in range(first, first + joint)]
                lane = slab_of(device) * share + first * rows
                finish(pl.ds(pl.multiple_of(lane, BLK), joint * rows), jnp.concatenate(pieces, axis=0))

    else:

        @pl.loop(1, n)
        def _(k):
            copy_back(0, me, peer(k)).wait_recv()

        @pl.loop(0, n // joint)
        def _(tile):
            slabs = [tile * joint + index for index in range(joint)]
            pieces = [back[0, lax.rem(slab, stretch) * ctx + slab // stretch] for slab in slabs]
            finish(pl.ds(pl.multiple_of(tile * BLK, BLK), BLK), jnp.concatenate(pieces, axis=0))

    for chunk in range(chunks):

        @pl.loop(1, n)
        def _(k, chunk=chunk):
            if chunk + 2 >= chunks:
                copy_in(chunk, peer(k), me).wait_send()
            copy_back(chunk, peer(k), me).wait_send()


def per_device(stretch, ctx, post_gate, pre_gate, values, filters, skip_bias, doc_blocks):
    n = stretch * ctx
    tok_rows, model = values.shape
    taps = filters.shape[1]
    share = model // n
    groups = filters.shape[0] // stretch
    width = share // groups
    blocks = n * tok_rows // BLK
    longest = blocks * 3 // 8
    lags = min(longest, taps // BLK + 1)
    chunks = share // (2 * width) if share % BLK == 0 else 1
    rows = share // chunks
    slab = (chunks, n, rows, BLK)
    vmem = pl.BlockSpec(memory_space=pltpu.VMEM)
    sems = pltpu.SemaphoreType.DMA((chunks, n))
    returned = pl.pallas_call(
        functools.partial(kernel, stretch, ctx, chunks, lags, width),
        out_shape=jax.ShapeDtypeStruct((tok_rows, model), jnp.bfloat16),
        in_specs=[
            pl.BlockSpec(memory_space=pltpu.HBM),
            pl.BlockSpec(memory_space=pltpu.HBM),
            pl.BlockSpec(memory_space=pltpu.HBM),
            vmem,
            pl.BlockSpec(memory_space=pltpu.SMEM),
        ],
        out_specs=vmem,
        scratch_shapes=[
            pltpu.VMEM((tok_rows, model), jnp.bfloat16),
            pltpu.VMEM((tok_rows, model), jnp.bfloat16),
            pltpu.VMEM(filters.shape, jnp.float32),
            pltpu.VMEM(slab, jnp.bfloat16),
            pltpu.VMEM((chunks, lags - 1 + n, rows, BLK), jnp.bfloat16),
            pltpu.VMEM(slab, jnp.bfloat16),
            pltpu.VMEM(slab, jnp.bfloat16),
            pltpu.VMEM((groups, lags * BLK, BLK), jnp.bfloat16),
            pltpu.VMEM((stretch * share, BLK), jnp.float32),
            pltpu.VMEM((blocks, lags, 16, BLK), jnp.bfloat16),
            pltpu.SemaphoreType.DMA((3,)),
            sems, sems, sems, sems,
        ],
        compiler_params=pltpu.CompilerParams(
            collective_id=0, has_side_effects=True, vmem_limit_bytes=58 * 1024 * 1024
        ),
    )(pre_gate, values, filters, skip_bias, doc_blocks)
    return (post_gate.astype(jnp.float32) * returned.astype(jnp.float32)).astype(jnp.bfloat16)


def solution(mesh):
    rows = P(("stretch", "ctx"), None)
    body = functools.partial(per_device, mesh.shape["stretch"], mesh.shape["ctx"])
    return jax.shard_map(
        body,
        mesh=mesh,
        in_specs=(rows, rows, rows, P("ctx", None), P("ctx"), P()),
        out_specs=rows,
        check_vma=False,
    )
```

```python
import functools
import math

import jax
import jax.numpy as jnp
from jax import lax
from jax.experimental import pallas as pl
from jax.experimental.pallas import tpu as pltpu
from jax.sharding import PartitionSpec as P

BLK = 128
TILE_BLOCKS = 8
MESH = pl.DeviceIdType.MESH


def kernel(
    stretch, ctx, chunks, lags, width,
    pre_ref, val_ref, filt_ref, skip_ref, docs_ref, out_ref,
    pre, val, filt, gated, arrived, mixed, back, toeplitz, skips, live,
    load_sem, send_in, recv_in, send_back, recv_back,
):
    loads = [
        pltpu.make_async_copy(pre_ref, pre, load_sem.at[0]),
        pltpu.make_async_copy(val_ref, val, load_sem.at[1]),
        pltpu.make_async_copy(filt_ref, filt, load_sem.at[2]),
    ]
    for load in loads:
        load.start()
    part = lax.axis_index("stretch")
    n = stretch * ctx
    me = lax.axis_index("stretch") * ctx + lax.axis_index("ctx")
    rows = gated.shape[2]
    share = chunks * rows
    lead = lags - 1
    chunk_groups = rows // width
    stride = 5 if math.gcd(5, n) == 1 else 1

    def peer(k):
        return lax.rem(me + k * stride, n)

    def place(device):
        return (device // ctx, lax.rem(device, ctx))

    def slab_of(device):
        return lax.rem(device, ctx) * stretch + device // ctx

    barrier = pltpu.get_barrier_semaphore()

    @pl.loop(1, n)
    def _(k):
        pl.semaphore_signal(barrier, inc=1, device_id=place(peer(k)), device_id_type=MESH)

    def copy_in(chunk, device, slot):
        return pltpu.make_async_remote_copy(
            src_ref=gated.at[chunk, slab_of(device)],
            dst_ref=arrived.at[chunk, lead + slot],
            send_sem=send_in.at[chunk, device],
            recv_sem=recv_in.at[chunk, slot],
            device_id=place(device),
            device_id_type=MESH,
        )

    def copy_back(chunk, device, slot):
        return pltpu.make_async_remote_copy(
            src_ref=mixed.at[chunk, device],
            dst_ref=back.at[chunk, slot],
            send_sem=send_back.at[chunk, device],
            recv_sem=recv_back.at[chunk, slot],
            device_id=place(device),
            device_id_type=MESH,
        )

    unit = max(share, BLK)
    per_unit = unit // share

    def gate(tile):
        lanes = pl.ds(pl.multiple_of(tile * unit, unit), unit)
        product = pre[:, lanes].astype(jnp.float32) * val[:, lanes].astype(jnp.float32)
        turned = product.T.astype(jnp.bfloat16)
        for slab in range(per_unit):
            for chunk in range(chunks):
                first = slab * share + chunk * rows
                gated[chunk, tile * per_unit + slab] = turned[first : first + rows]

    for load in loads[:2]:
        load.wait()
    early = n // 4 if per_unit == 1 else n

    if per_unit == 1:

        @pl.loop(0, early)
        def _(k):
            gate(slab_of(peer(k)))

    else:

        @pl.loop(0, n // per_unit)
        def _(tile):
            gate(tile)

    pl.semaphore_wait(barrier, n - 1)

    @pl.loop(1, early)
    def _(k):
        copy_in(0, peer(k), me).start()

    @pl.loop(early, n)
    def _(k):
        gate(slab_of(peer(k)))
        copy_in(0, peer(k), me).start()

    for chunk in range(chunks):
        arrived[chunk, lead + me] = gated[chunk, slab_of(me)]
        arrived[chunk, 0:lead] = jnp.zeros((lead, rows, BLK), jnp.bfloat16)

    loads[2].wait()
    taps = filt.shape[1]

    @pl.loop(0, chunks * chunk_groups)
    def _(group):
        row = part * (chunks * chunk_groups) + group
        chosen = lax.broadcasted_iota(jnp.int32, (filt.shape[0], BLK), 0) == row
        for lag in range(lags):
            pieces = []
            for first in ((lag - 1) * BLK, lag * BLK):
                if 0 <= first < taps:
                    picked = jnp.where(chosen, filt[:, first : first + BLK], 0.0)
                    pieces.append(jnp.sum(picked, axis=0, keepdims=True))
                else:
                    pieces.append(jnp.zeros((1, BLK), jnp.float32))
            spread = jnp.broadcast_to(jnp.concatenate(pieces, axis=1), (BLK, 2 * BLK))
            turned = pltpu.roll(spread, 0, 1, stride=1, stride_axis=0)
            toeplitz[group, lag * BLK : (lag + 1) * BLK, :] = turned[:, BLK:].astype(jnp.bfloat16)

    skips[...] = jnp.broadcast_to(skip_ref[...].reshape(1, stretch * share), (BLK, stretch * share)).T
    ends = []
    for doc in range(docs_ref.shape[0]):
        ends.append(docs_ref[doc] + (ends[-1] if ends else 0))

    @pl.loop(0, n)
    def _(block):
        start = jnp.int32(0)
        for end in ends:
            start = jnp.maximum(start, jnp.where(end <= block, end, 0))
        for lag in range(lags):
            weight = jnp.where(block - lag >= start, 1.0, 0.0).astype(jnp.float32)
            live[block, lag] = jnp.full(live.shape[2:], weight, jnp.float32).astype(jnp.bfloat16)

    for chunk in range(1, chunks):

        @pl.loop(1, n)
        def _(k, chunk=chunk):
            copy_in(chunk - 1, peer(k), me).wait_send()
            copy_in(chunk, peer(k), me).start()

    for chunk in range(chunks):

        @pl.loop(1, n)
        def _(k, chunk=chunk):
            copy_in(chunk, me, peer(k)).wait_recv()

        @pl.loop(0, chunk_groups * (n // TILE_BLOCKS))
        def _(step, chunk=chunk):
            group = step // (n // TILE_BLOCKS)
            first = lax.rem(step, n // TILE_BLOCKS) * TILE_BLOCKS
            channels = pl.ds(pl.multiple_of(group * width, width), width)
            columns = []
            for lag in range(lags):
                pieces = []
                for block in range(TILE_BLOCKS):
                    source = first + (lead + block - lag)
                    kept = jnp.concatenate([live[first + block, lag]] * (width // live.shape[2]), axis=0)
                    pieces.append(arrived[chunk, source, channels, :] * kept)
                columns.append(jnp.concatenate(pieces, axis=0))
            window = jnp.concatenate(columns, axis=1)
            conv = jnp.dot(
                window, toeplitz[chunk * chunk_groups + group], preferred_element_type=jnp.float32
            )
            skip_row = part * share + chunk * rows + group * width
            skip = skips[pl.ds(pl.multiple_of(skip_row, width), width), :]
            for block in range(TILE_BLOCKS):
                direct = arrived[chunk, first + (lead + block), channels, :].astype(jnp.float32)
                total = conv[block * width : (block + 1) * width] + skip * direct
                mixed[chunk, first + block, channels, :] = total.astype(jnp.bfloat16)

        back[chunk, me] = mixed[chunk, me]

        @pl.loop(1, n)
        def _(k, chunk=chunk):
            if chunk == 0:
                copy_in(chunks - 1, peer(k), me).wait_send()
            copy_back(chunk, peer(k), me).start()

    def finish(lanes, turned):
        out_ref[:, lanes] = turned.astype(jnp.float32).T.astype(jnp.bfloat16)

    joint = max(BLK // rows, 1)
    if share % BLK == 0:
        for first in range(0, chunks, joint):

            @pl.loop(0, n)
            def _(k, first=first):
                device = peer(k)

                @pl.when(k > 0)
                def _():
                    for chunk in range(first, first + joint):
                        copy_back(chunk, me, device).wait_recv()

                pieces = [back[chunk, device] for chunk in range(first, first + joint)]
                lane = slab_of(device) * share + first * rows
                finish(pl.ds(pl.multiple_of(lane, BLK), joint * rows), jnp.concatenate(pieces, axis=0))

    else:

        @pl.loop(1, n)
        def _(k):
            copy_back(0, me, peer(k)).wait_recv()

        @pl.loop(0, n // joint)
        def _(tile):
            slabs = [tile * joint + index for index in range(joint)]
            pieces = [back[0, lax.rem(slab, stretch) * ctx + slab // stretch] for slab in slabs]
            finish(pl.ds(pl.multiple_of(tile * BLK, BLK), BLK), jnp.concatenate(pieces, axis=0))

    for chunk in range(chunks):

        @pl.loop(1, n)
        def _(k, chunk=chunk):
            copy_back(chunk, peer(k), me).wait_send()


def per_device(stretch, ctx, post_gate, pre_gate, values, filters, skip_bias, doc_blocks):
    n = stretch * ctx
    tok_rows, model = values.shape
    taps = filters.shape[1]
    share = model // n
    groups = filters.shape[0] // stretch
    width = share // groups
    blocks = n * tok_rows // BLK
    longest = blocks * 3 // 8
    lags = min(longest, taps // BLK + 1)
    chunks = share // BLK if share % BLK == 0 else 1
    rows = share // chunks
    slab = (chunks, n, rows, BLK)
    vmem = pl.BlockSpec(memory_space=pltpu.VMEM)
    sems = pltpu.SemaphoreType.DMA((chunks, n))
    returned = pl.pallas_call(
        functools.partial(kernel, stretch, ctx, chunks, lags, width),
        out_shape=jax.ShapeDtypeStruct((tok_rows, model), jnp.bfloat16),
        in_specs=[
            pl.BlockSpec(memory_space=pltpu.HBM),
            pl.BlockSpec(memory_space=pltpu.HBM),
            pl.BlockSpec(memory_space=pltpu.HBM),
            vmem,
            pl.BlockSpec(memory_space=pltpu.SMEM),
        ],
        out_specs=vmem,
        scratch_shapes=[
            pltpu.VMEM((tok_rows, model), jnp.bfloat16),
            pltpu.VMEM((tok_rows, model), jnp.bfloat16),
            pltpu.VMEM(filters.shape, jnp.float32),
            pltpu.VMEM(slab, jnp.bfloat16),
            pltpu.VMEM((chunks, lags - 1 + n, rows, BLK), jnp.bfloat16),
            pltpu.VMEM(slab, jnp.bfloat16),
            pltpu.VMEM(slab, jnp.bfloat16),
            pltpu.VMEM((groups, lags * BLK, BLK), jnp.bfloat16),
            pltpu.VMEM((stretch * share, BLK), jnp.float32),
            pltpu.VMEM((blocks, lags, 16, BLK), jnp.bfloat16),
            pltpu.SemaphoreType.DMA((3,)),
            sems, sems, sems, sems,
        ],
        compiler_params=pltpu.CompilerParams(
            collective_id=0, has_side_effects=True, vmem_limit_bytes=58 * 1024 * 1024
        ),
    )(pre_gate, values, filters, skip_bias, doc_blocks)
    return (post_gate.astype(jnp.float32) * returned.astype(jnp.float32)).astype(jnp.bfloat16)


def solution(mesh):
    rows = P(("stretch", "ctx"), None)
    body = functools.partial(per_device, mesh.shape["stretch"], mesh.shape["ctx"])
    return jax.shard_map(
        body,
        mesh=mesh,
        in_specs=(rows, rows, rows, P("ctx", None), P("ctx"), P()),
        out_specs=rows,
        check_vma=False,
    )
```

```python
import functools
import math

import jax
import jax.numpy as jnp
from jax import lax
from jax.experimental import pallas as pl
from jax.experimental.pallas import tpu as pltpu
from jax.sharding import PartitionSpec as P

BLK = 128
TILE_BLOCKS = 8
GATE_STEPS = 4
MESH = pl.DeviceIdType.MESH


def kernel(
    stretch, ctx, chunks, lags, width,
    pre_ref, val_ref, filt_ref, skip_ref, docs_ref, out_ref,
    pre, val, filt, gated, arrived, mixed, back, toeplitz, skips, live,
    load_sem, pre_sem, val_sem, send_in, recv_in, send_back, recv_back,
):
    filter_load = pltpu.make_async_copy(filt_ref, filt, load_sem)
    filter_load.start()
    part = lax.axis_index("stretch")
    n = stretch * ctx
    me = lax.axis_index("stretch") * ctx + lax.axis_index("ctx")
    rows = gated.shape[2]
    share = chunks * rows
    lead = lags - 1
    chunk_groups = rows // width
    stride = 5 if math.gcd(5, n) == 1 else 1

    def peer(k):
        return lax.rem(me + k * stride, n)

    def place(device):
        return (device // ctx, lax.rem(device, ctx))

    def slab_of(device):
        return lax.rem(device, ctx) * stretch + device // ctx

    unit = max(share, BLK)
    per_unit = unit // share

    tiles = n // per_unit

    def tile_at(turn):
        return slab_of(peer(turn)) if per_unit == 1 else turn

    def tile_loads(turn):
        lanes = pl.ds(pl.multiple_of(tile_at(turn) * unit, unit), unit)
        return (
            pltpu.make_async_copy(pre_ref.at[:, lanes], pre.at[:, lanes], pre_sem.at[turn]),
            pltpu.make_async_copy(val_ref.at[:, lanes], val.at[:, lanes], val_sem.at[turn]),
        )

    early = n // 8 if per_unit == 1 else n
    barrier = pltpu.get_barrier_semaphore()

    @pl.loop(0, min(early, tiles))
    def _(turn):
        for load in tile_loads(turn):
            load.start()

    @pl.loop(1, n)
    def _(k):
        pl.semaphore_signal(barrier, inc=1, device_id=place(peer(k)), device_id_type=MESH)

    @pl.loop(min(early, tiles), tiles)
    def _(turn):
        for load in tile_loads(turn):
            load.start()

    def copy_in(chunk, device, slot):
        return pltpu.make_async_remote_copy(
            src_ref=gated.at[chunk, slab_of(device)],
            dst_ref=arrived.at[chunk, lead + slot],
            send_sem=send_in.at[chunk, device],
            recv_sem=recv_in.at[chunk, slot],
            device_id=place(device),
            device_id_type=MESH,
        )

    def copy_back(chunk, device, slot):
        return pltpu.make_async_remote_copy(
            src_ref=mixed.at[chunk, device],
            dst_ref=back.at[chunk, slot],
            send_sem=send_back.at[chunk, device],
            recv_sem=recv_back.at[chunk, slot],
            device_id=place(device),
            device_id_type=MESH,
        )

    def gate(turn):
        for load in tile_loads(turn):
            load.wait()
        tile = tile_at(turn)
        lanes = pl.ds(pl.multiple_of(tile * unit, unit), unit)
        product = pre[:, lanes].astype(jnp.float32) * val[:, lanes].astype(jnp.float32)
        turned = product.T.astype(jnp.bfloat16)
        for slab in range(per_unit):
            for chunk in range(chunks):
                first = slab * share + chunk * rows
                gated[chunk, tile * per_unit + slab] = turned[first : first + rows]

    @pl.loop(0, min(early, tiles))
    def _(turn):
        gate(turn)

    pl.semaphore_wait(barrier, n - 1)

    @pl.loop(1, early)
    def _(k):
        copy_in(0, peer(k), me).start()

    @pl.loop(early, n)
    def _(k):
        gate(k)
        copy_in(0, peer(k), me).start()

    for chunk in range(chunks):
        arrived[chunk, lead + me] = gated[chunk, slab_of(me)]
        arrived[chunk, 0:lead] = jnp.zeros((lead, rows, BLK), jnp.bfloat16)

    filter_load.wait()
    taps = filt.shape[1]

    @pl.loop(0, chunks * chunk_groups)
    def _(group):
        row = part * (chunks * chunk_groups) + group
        chosen = lax.broadcasted_iota(jnp.int32, (filt.shape[0], BLK), 0) == row
        for lag in range(lags):
            pieces = []
            for first in ((lag - 1) * BLK, lag * BLK):
                if 0 <= first < taps:
                    picked = jnp.where(chosen, filt[:, first : first + BLK], 0.0)
                    pieces.append(jnp.sum(picked, axis=0, keepdims=True))
                else:
                    pieces.append(jnp.zeros((1, BLK), jnp.float32))
            spread = jnp.broadcast_to(jnp.concatenate(pieces, axis=1), (BLK, 2 * BLK))
            turned = pltpu.roll(spread, 0, 1, stride=1, stride_axis=0)
            toeplitz[group, lag * BLK : (lag + 1) * BLK, :] = turned[:, BLK:].astype(jnp.bfloat16)

    skips[...] = jnp.broadcast_to(skip_ref[...].reshape(1, stretch * share), (BLK, stretch * share)).T
    ends = []
    for doc in range(docs_ref.shape[0]):
        ends.append(docs_ref[doc] + (ends[-1] if ends else 0))

    @pl.loop(0, n)
    def _(block):
        start = jnp.int32(0)
        for end in ends:
            start = jnp.maximum(start, jnp.where(end <= block, end, 0))
        for lag in range(lags):
            weight = jnp.where(block - lag >= start, 1.0, 0.0).astype(jnp.float32)
            live[block, lag] = jnp.full(live.shape[2:], weight, jnp.float32).astype(jnp.bfloat16)

    for chunk in range(1, chunks):

        @pl.loop(1, n)
        def _(k, chunk=chunk):
            copy_in(chunk - 1, peer(k), me).wait_send()
            copy_in(chunk, peer(k), me).start()

    for chunk in range(chunks):

        @pl.loop(1, n)
        def _(k, chunk=chunk):
            copy_in(chunk, me, peer(k)).wait_recv()

        @pl.loop(0, chunk_groups * (n // TILE_BLOCKS))
        def _(step, chunk=chunk):
            group = step // (n // TILE_BLOCKS)
            first = lax.rem(step, n // TILE_BLOCKS) * TILE_BLOCKS
            channels = pl.ds(pl.multiple_of(group * width, width), width)
            columns = []
            for lag in range(lags):
                pieces = []
                for block in range(TILE_BLOCKS):
                    source = first + (lead + block - lag)
                    kept = jnp.concatenate([live[first + block, lag]] * (width // live.shape[2]), axis=0)
                    pieces.append(arrived[chunk, source, channels, :] * kept)
                columns.append(jnp.concatenate(pieces, axis=0))
            window = jnp.concatenate(columns, axis=1)
            conv = jnp.dot(
                window, toeplitz[chunk * chunk_groups + group], preferred_element_type=jnp.float32
            )
            skip_row = part * share + chunk * rows + group * width
            skip = skips[pl.ds(pl.multiple_of(skip_row, width), width), :]
            for block in range(TILE_BLOCKS):
                direct = arrived[chunk, first + (lead + block), channels, :].astype(jnp.float32)
                total = conv[block * width : (block + 1) * width] + skip * direct
                mixed[chunk, first + block, channels, :] = total.astype(jnp.bfloat16)

        back[chunk, me] = mixed[chunk, me]

        @pl.loop(1, n)
        def _(k, chunk=chunk):
            if chunk == 0:
                copy_in(chunks - 1, peer(k), me).wait_send()
            copy_back(chunk, peer(k), me).start()

    def finish(lanes, turned):
        out_ref[:, lanes] = turned.astype(jnp.float32).T.astype(jnp.bfloat16)

    joint = max(BLK // rows, 1)
    if share % BLK == 0:
        for first in range(0, chunks, joint):

            @pl.loop(0, n)
            def _(k, first=first):
                device = peer(k)

                @pl.when(k > 0)
                def _():
                    for chunk in range(first, first + joint):
                        copy_back(chunk, me, device).wait_recv()

                pieces = [back[chunk, device] for chunk in range(first, first + joint)]
                lane = slab_of(device) * share + first * rows
                finish(pl.ds(pl.multiple_of(lane, BLK), joint * rows), jnp.concatenate(pieces, axis=0))

    else:

        @pl.loop(1, n)
        def _(k):
            copy_back(0, me, peer(k)).wait_recv()

        @pl.loop(0, n // joint)
        def _(tile):
            slabs = [tile * joint + index for index in range(joint)]
            pieces = [back[0, lax.rem(slab, stretch) * ctx + slab // stretch] for slab in slabs]
            finish(pl.ds(pl.multiple_of(tile * BLK, BLK), BLK), jnp.concatenate(pieces, axis=0))

    for chunk in range(chunks):

        @pl.loop(1, n)
        def _(k, chunk=chunk):
            copy_back(chunk, peer(k), me).wait_send()


def gate_kernel(post_ref, mixed_ref, out_ref):
    product = post_ref[...].astype(jnp.float32) * mixed_ref[...].astype(jnp.float32)
    out_ref[...] = product.astype(jnp.bfloat16)


def per_device(stretch, ctx, post_gate, pre_gate, values, filters, skip_bias, doc_blocks):
    n = stretch * ctx
    tok_rows, model = values.shape
    taps = filters.shape[1]
    share = model // n
    groups = filters.shape[0] // stretch
    width = share // groups
    blocks = n * tok_rows // BLK
    longest = blocks * 3 // 8
    lags = min(longest, taps // BLK + 1)
    chunks = share // BLK if share % BLK == 0 else 1
    rows = share // chunks
    slab = (chunks, n, rows, BLK)
    vmem = pl.BlockSpec(memory_space=pltpu.VMEM)
    sems = pltpu.SemaphoreType.DMA((chunks, n))
    returned = pl.pallas_call(
        functools.partial(kernel, stretch, ctx, chunks, lags, width),
        out_shape=jax.ShapeDtypeStruct((tok_rows, model), jnp.bfloat16),
        in_specs=[
            pl.BlockSpec(memory_space=pltpu.HBM),
            pl.BlockSpec(memory_space=pltpu.HBM),
            pl.BlockSpec(memory_space=pltpu.HBM),
            vmem,
            pl.BlockSpec(memory_space=pltpu.SMEM),
        ],
        out_specs=vmem,
        scratch_shapes=[
            pltpu.VMEM((tok_rows, model), jnp.bfloat16),
            pltpu.VMEM((tok_rows, model), jnp.bfloat16),
            pltpu.VMEM(filters.shape, jnp.float32),
            pltpu.VMEM(slab, jnp.bfloat16),
            pltpu.VMEM((chunks, lags - 1 + n, rows, BLK), jnp.bfloat16),
            pltpu.VMEM(slab, jnp.bfloat16),
            pltpu.VMEM(slab, jnp.bfloat16),
            pltpu.VMEM((groups, lags * BLK, BLK), jnp.bfloat16),
            pltpu.VMEM((stretch * share, BLK), jnp.float32),
            pltpu.VMEM((blocks, lags, 16, BLK), jnp.bfloat16),
            pltpu.SemaphoreType.DMA(()),
            pltpu.SemaphoreType.DMA((n,)),
            pltpu.SemaphoreType.DMA((n,)),
            sems, sems, sems, sems,
        ],
        compiler_params=pltpu.CompilerParams(
            collective_id=0, has_side_effects=True, vmem_limit_bytes=58 * 1024 * 1024
        ),
    )(pre_gate, values, filters, skip_bias, doc_blocks)
    block = pl.BlockSpec((tok_rows // GATE_STEPS, model), lambda step: (step, 0))
    return pl.pallas_call(
        gate_kernel,
        out_shape=jax.ShapeDtypeStruct((tok_rows, model), jnp.bfloat16),
        grid=(GATE_STEPS,),
        in_specs=[block, block],
        out_specs=block,
        compiler_params=pltpu.CompilerParams(vmem_limit_bytes=58 * 1024 * 1024),
    )(post_gate, returned)


def solution(mesh):
    rows = P(("stretch", "ctx"), None)
    body = functools.partial(per_device, mesh.shape["stretch"], mesh.shape["ctx"])
    return jax.shard_map(
        body,
        mesh=mesh,
        in_specs=(rows, rows, rows, P("ctx", None), P("ctx"), P()),
        out_specs=rows,
        check_vma=False,
    )
```

```python
import functools
import math

import jax
import jax.numpy as jnp
from jax import lax
from jax.experimental import pallas as pl
from jax.experimental.pallas import tpu as pltpu
from jax.sharding import PartitionSpec as P

BLK = 128
TILE_BLOCKS = 8
MESH = pl.DeviceIdType.MESH


def kernel(
    stretch, ctx, chunks, lags, width,
    pre_ref, val_ref, filt_ref, skip_ref, docs_ref, out_ref,
    pre, val, filt, gated, arrived, mixed, back, toeplitz, skips, live,
    load_sem, send_in, recv_in, send_back, recv_back,
):
    loads = [
        pltpu.make_async_copy(pre_ref, pre, load_sem.at[0]),
        pltpu.make_async_copy(val_ref, val, load_sem.at[1]),
        pltpu.make_async_copy(filt_ref, filt, load_sem.at[2]),
    ]
    for load in loads:
        load.start()
    part = lax.axis_index("stretch")
    n = stretch * ctx
    me = lax.axis_index("stretch") * ctx + lax.axis_index("ctx")
    rows = gated.shape[2]
    share = chunks * rows
    lead = lags - 1
    chunk_groups = rows // width
    stride = 5 if math.gcd(5, n) == 1 else 1

    def peer(k):
        return lax.rem(me + k * stride, n)

    def place(device):
        return (device // ctx, lax.rem(device, ctx))

    def slab_of(device):
        return lax.rem(device, ctx) * stretch + device // ctx

    barrier = pltpu.get_barrier_semaphore()

    @pl.loop(1, n)
    def _(k):
        pl.semaphore_signal(barrier, inc=1, device_id=place(peer(k)), device_id_type=MESH)

    def copy_in(chunk, device, slot):
        return pltpu.make_async_remote_copy(
            src_ref=gated.at[chunk, slab_of(device)],
            dst_ref=arrived.at[chunk, lead + slot],
            send_sem=send_in.at[chunk, device],
            recv_sem=recv_in.at[chunk, slot],
            device_id=place(device),
            device_id_type=MESH,
        )

    def copy_back(chunk, device, slot):
        return pltpu.make_async_remote_copy(
            src_ref=mixed.at[chunk, device],
            dst_ref=back.at[chunk, slot],
            send_sem=send_back.at[chunk, device],
            recv_sem=recv_back.at[chunk, slot],
            device_id=place(device),
            device_id_type=MESH,
        )

    unit = max(share, BLK)
    per_unit = unit // share

    def gate(tile):
        lanes = pl.ds(pl.multiple_of(tile * unit, unit), unit)
        product = pre[:, lanes].astype(jnp.float32) * val[:, lanes].astype(jnp.float32)
        turned = product.T.astype(jnp.bfloat16)
        for slab in range(per_unit):
            for chunk in range(chunks):
                first = slab * share + chunk * rows
                gated[chunk, tile * per_unit + slab] = turned[first : first + rows]

    for load in loads[:2]:
        load.wait()
    early = n // 4 if per_unit == 1 else n

    if per_unit == 1:

        @pl.loop(0, early)
        def _(k):
            gate(slab_of(peer(k)))

    else:

        @pl.loop(0, n // per_unit)
        def _(tile):
            gate(tile)

    pl.semaphore_wait(barrier, n - 1)

    @pl.loop(1, early)
    def _(k):
        copy_in(0, peer(k), me).start()

    @pl.loop(early, n)
    def _(k):
        gate(slab_of(peer(k)))
        copy_in(0, peer(k), me).start()

    for chunk in range(1, chunks):

        @pl.loop(1, n)
        def _(k, chunk=chunk):
            copy_in(chunk, peer(k), me).start()

    for chunk in range(chunks):
        arrived[chunk, lead + me] = gated[chunk, slab_of(me)]
        arrived[chunk, 0:lead] = jnp.zeros((lead, rows, BLK), jnp.bfloat16)

    loads[2].wait()
    taps = filt.shape[1]

    @pl.loop(0, chunks * chunk_groups)
    def _(group):
        row = part * (chunks * chunk_groups) + group
        chosen = lax.broadcasted_iota(jnp.int32, (filt.shape[0], BLK), 0) == row
        for lag in range(lags):
            pieces = []
            for first in ((lag - 1) * BLK, lag * BLK):
                if 0 <= first < taps:
                    picked = jnp.where(chosen, filt[:, first : first + BLK], 0.0)
                    pieces.append(jnp.sum(picked, axis=0, keepdims=True))
                else:
                    pieces.append(jnp.zeros((1, BLK), jnp.float32))
            spread = jnp.broadcast_to(jnp.concatenate(pieces, axis=1), (BLK, 2 * BLK))
            turned = pltpu.roll(spread, 0, 1, stride=1, stride_axis=0)
            toeplitz[group, lag * BLK : (lag + 1) * BLK, :] = turned[:, BLK:].astype(jnp.bfloat16)

    skips[...] = jnp.broadcast_to(skip_ref[...].reshape(1, stretch * share), (BLK, stretch * share)).T
    ends = []
    for doc in range(docs_ref.shape[0]):
        ends.append(docs_ref[doc] + (ends[-1] if ends else 0))

    @pl.loop(0, n)
    def _(block):
        start = jnp.int32(0)
        for end in ends:
            start = jnp.maximum(start, jnp.where(end <= block, end, 0))
        for lag in range(lags):
            weight = jnp.where(block - lag >= start, 1.0, 0.0).astype(jnp.float32)
            live[block, lag] = jnp.full(live.shape[2:], weight, jnp.float32).astype(jnp.bfloat16)

    for chunk in range(chunks):

        @pl.loop(1, n)
        def _(k, chunk=chunk):
            copy_in(chunk, me, peer(k)).wait_recv()

        @pl.loop(0, chunk_groups * (n // TILE_BLOCKS))
        def _(step, chunk=chunk):
            group = step // (n // TILE_BLOCKS)
            first = lax.rem(step, n // TILE_BLOCKS) * TILE_BLOCKS
            channels = pl.ds(pl.multiple_of(group * width, width), width)
            columns = []
            for lag in range(lags):
                pieces = []
                for block in range(TILE_BLOCKS):
                    source = first + (lead + block - lag)
                    kept = jnp.concatenate([live[first + block, lag]] * (width // live.shape[2]), axis=0)
                    pieces.append(arrived[chunk, source, channels, :] * kept)
                columns.append(jnp.concatenate(pieces, axis=0))
            window = jnp.concatenate(columns, axis=1)
            conv = jnp.dot(
                window, toeplitz[chunk * chunk_groups + group], preferred_element_type=jnp.float32
            )
            skip_row = part * share + chunk * rows + group * width
            skip = skips[pl.ds(pl.multiple_of(skip_row, width), width), :]
            for block in range(TILE_BLOCKS):
                direct = arrived[chunk, first + (lead + block), channels, :].astype(jnp.float32)
                total = conv[block * width : (block + 1) * width] + skip * direct
                mixed[chunk, first + block, channels, :] = total.astype(jnp.bfloat16)

        back[chunk, me] = mixed[chunk, me]

        @pl.loop(1, n)
        def _(k, chunk=chunk):
            copy_back(chunk, peer(k), me).start()

    def finish(lanes, turned):
        out_ref[:, lanes] = turned.astype(jnp.float32).T.astype(jnp.bfloat16)

    joint = max(BLK // rows, 1)
    if share % BLK == 0:
        for first in range(0, chunks, joint):

            @pl.loop(0, n)
            def _(k, first=first):
                device = peer(k)

                @pl.when(k > 0)
                def _():
                    for chunk in range(first, first + joint):
                        copy_back(chunk, me, device).wait_recv()

                pieces = [back[chunk, device] for chunk in range(first, first + joint)]
                lane = slab_of(device) * share + first * rows
                finish(pl.ds(pl.multiple_of(lane, BLK), joint * rows), jnp.concatenate(pieces, axis=0))

    else:

        @pl.loop(1, n)
        def _(k):
            copy_back(0, me, peer(k)).wait_recv()

        @pl.loop(0, n // joint)
        def _(tile):
            slabs = [tile * joint + index for index in range(joint)]
            pieces = [back[0, lax.rem(slab, stretch) * ctx + slab // stretch] for slab in slabs]
            finish(pl.ds(pl.multiple_of(tile * BLK, BLK), BLK), jnp.concatenate(pieces, axis=0))

    for chunk in range(chunks):

        @pl.loop(1, n)
        def _(k, chunk=chunk):
            copy_in(chunk, peer(k), me).wait_send()
            copy_back(chunk, peer(k), me).wait_send()


def per_device(stretch, ctx, post_gate, pre_gate, values, filters, skip_bias, doc_blocks):
    n = stretch * ctx
    tok_rows, model = values.shape
    taps = filters.shape[1]
    share = model // n
    groups = filters.shape[0] // stretch
    width = share // groups
    blocks = n * tok_rows // BLK
    longest = blocks * 3 // 8
    lags = min(longest, taps // BLK + 1)
    chunks = share // BLK if share % BLK == 0 else 1
    rows = share // chunks
    slab = (chunks, n, rows, BLK)
    vmem = pl.BlockSpec(memory_space=pltpu.VMEM)
    sems = pltpu.SemaphoreType.DMA((chunks, n))
    returned = pl.pallas_call(
        functools.partial(kernel, stretch, ctx, chunks, lags, width),
        out_shape=jax.ShapeDtypeStruct((tok_rows, model), jnp.bfloat16),
        in_specs=[
            pl.BlockSpec(memory_space=pltpu.HBM),
            pl.BlockSpec(memory_space=pltpu.HBM),
            pl.BlockSpec(memory_space=pltpu.HBM),
            vmem,
            pl.BlockSpec(memory_space=pltpu.SMEM),
        ],
        out_specs=vmem,
        scratch_shapes=[
            pltpu.VMEM((tok_rows, model), jnp.bfloat16),
            pltpu.VMEM((tok_rows, model), jnp.bfloat16),
            pltpu.VMEM(filters.shape, jnp.float32),
            pltpu.VMEM(slab, jnp.bfloat16),
            pltpu.VMEM((chunks, lags - 1 + n, rows, BLK), jnp.bfloat16),
            pltpu.VMEM(slab, jnp.bfloat16),
            pltpu.VMEM(slab, jnp.bfloat16),
            pltpu.VMEM((groups, lags * BLK, BLK), jnp.bfloat16),
            pltpu.VMEM((stretch * share, BLK), jnp.float32),
            pltpu.VMEM((blocks, lags, 16, BLK), jnp.bfloat16),
            pltpu.SemaphoreType.DMA((3,)),
            sems, sems, sems, sems,
        ],
        compiler_params=pltpu.CompilerParams(
            collective_id=0, has_side_effects=True, vmem_limit_bytes=58 * 1024 * 1024
        ),
    )(pre_gate, values, filters, skip_bias, doc_blocks)
    return (post_gate.astype(jnp.float32) * returned.astype(jnp.float32)).astype(jnp.bfloat16)


def solution(mesh):
    rows = P(("stretch", "ctx"), None)
    body = functools.partial(per_device, mesh.shape["stretch"], mesh.shape["ctx"])
    return jax.shard_map(
        body,
        mesh=mesh,
        in_specs=(rows, rows, rows, P("ctx", None), P("ctx"), P()),
        out_specs=rows,
        check_vma=False,
    )
```

```python
import functools
import math

import jax
import jax.numpy as jnp
from jax import lax
from jax.experimental import pallas as pl
from jax.experimental.pallas import tpu as pltpu
from jax.sharding import PartitionSpec as P

BLK = 128
TILE_BLOCKS = 8
MESH = pl.DeviceIdType.MESH


def kernel(
    stretch, ctx, chunks, lags, width,
    pre_ref, val_ref, post_ref, filt_ref, skip_ref, docs_ref, out_ref,
    pre, val, post, filt, gated, arrived, mixed, back, toeplitz, skips, live,
    load_sem, send_in, recv_in, send_back, recv_back,
):
    loads = [
        pltpu.make_async_copy(pre_ref, pre, load_sem.at[0]),
        pltpu.make_async_copy(val_ref, val, load_sem.at[1]),
        pltpu.make_async_copy(filt_ref, filt, load_sem.at[2]),
        pltpu.make_async_copy(post_ref, post, load_sem.at[3]),
    ]
    for load in loads:
        load.start()
    part = lax.axis_index("stretch")
    n = stretch * ctx
    me = lax.axis_index("stretch") * ctx + lax.axis_index("ctx")
    rows = gated.shape[2]
    share = chunks * rows
    lead = lags - 1
    chunk_groups = rows // width
    stride = 5 if math.gcd(5, n) == 1 else 1

    def peer(k):
        return lax.rem(me + k * stride, n)

    def place(device):
        return (device // ctx, lax.rem(device, ctx))

    def slab_of(device):
        return lax.rem(device, ctx) * stretch + device // ctx

    barrier = pltpu.get_barrier_semaphore()

    @pl.loop(1, n)
    def _(k):
        pl.semaphore_signal(barrier, inc=1, device_id=place(peer(k)), device_id_type=MESH)

    def copy_in(chunk, device, slot):
        return pltpu.make_async_remote_copy(
            src_ref=gated.at[chunk, slab_of(device)],
            dst_ref=arrived.at[chunk, lead + slot],
            send_sem=send_in.at[chunk, device],
            recv_sem=recv_in.at[chunk, slot],
            device_id=place(device),
            device_id_type=MESH,
        )

    def copy_back(chunk, device, slot):
        return pltpu.make_async_remote_copy(
            src_ref=mixed.at[chunk, device],
            dst_ref=back.at[chunk, slot],
            send_sem=send_back.at[chunk, device],
            recv_sem=recv_back.at[chunk, slot],
            device_id=place(device),
            device_id_type=MESH,
        )

    unit = max(share, BLK)
    per_unit = unit // share

    def gate(tile):
        lanes = pl.ds(pl.multiple_of(tile * unit, unit), unit)
        product = pre[:, lanes].astype(jnp.float32) * val[:, lanes].astype(jnp.float32)
        turned = product.T.astype(jnp.bfloat16)
        for slab in range(per_unit):
            for chunk in range(chunks):
                first = slab * share + chunk * rows
                gated[chunk, tile * per_unit + slab] = turned[first : first + rows]

    for load in loads[:2]:
        load.wait()
    early = n // 4 if per_unit == 1 else n

    if per_unit == 1:

        @pl.loop(0, early)
        def _(k):
            gate(slab_of(peer(k)))

    else:

        @pl.loop(0, n // per_unit)
        def _(tile):
            gate(tile)

    pl.semaphore_wait(barrier, n - 1)

    @pl.loop(1, early)
    def _(k):
        copy_in(0, peer(k), me).start()

    @pl.loop(early, n)
    def _(k):
        gate(slab_of(peer(k)))
        copy_in(0, peer(k), me).start()

    for chunk in range(1, chunks):

        @pl.loop(1, n)
        def _(k, chunk=chunk):
            copy_in(chunk, peer(k), me).start()

    for chunk in range(chunks):
        arrived[chunk, lead + me] = gated[chunk, slab_of(me)]
        arrived[chunk, 0:lead] = jnp.zeros((lead, rows, BLK), jnp.bfloat16)

    loads[2].wait()
    loads[3].wait()
    taps = filt.shape[1]

    @pl.loop(0, chunks * chunk_groups)
    def _(group):
        row = part * (chunks * chunk_groups) + group
        chosen = lax.broadcasted_iota(jnp.int32, (filt.shape[0], BLK), 0) == row
        for lag in range(lags):
            pieces = []
            for first in ((lag - 1) * BLK, lag * BLK):
                if 0 <= first < taps:
                    picked = jnp.where(chosen, filt[:, first : first + BLK], 0.0)
                    pieces.append(jnp.sum(picked, axis=0, keepdims=True))
                else:
                    pieces.append(jnp.zeros((1, BLK), jnp.float32))
            spread = jnp.broadcast_to(jnp.concatenate(pieces, axis=1), (BLK, 2 * BLK))
            turned = pltpu.roll(spread, 0, 1, stride=1, stride_axis=0)
            toeplitz[group, lag * BLK : (lag + 1) * BLK, :] = turned[:, BLK:].astype(jnp.bfloat16)

    skips[...] = jnp.broadcast_to(skip_ref[...].reshape(1, stretch * share), (BLK, stretch * share)).T
    ends = []
    for doc in range(docs_ref.shape[0]):
        ends.append(docs_ref[doc] + (ends[-1] if ends else 0))

    @pl.loop(0, n)
    def _(block):
        start = jnp.int32(0)
        for end in ends:
            start = jnp.maximum(start, jnp.where(end <= block, end, 0))
        for lag in range(lags):
            weight = jnp.where(block - lag >= start, 1.0, 0.0).astype(jnp.float32)
            live[block, lag] = jnp.full(live.shape[2:], weight, jnp.float32).astype(jnp.bfloat16)

    for chunk in range(chunks):

        @pl.loop(1, n)
        def _(k, chunk=chunk):
            copy_in(chunk, me, peer(k)).wait_recv()

        @pl.loop(0, chunk_groups * (n // TILE_BLOCKS))
        def _(step, chunk=chunk):
            group = step // (n // TILE_BLOCKS)
            first = lax.rem(step, n // TILE_BLOCKS) * TILE_BLOCKS
            channels = pl.ds(pl.multiple_of(group * width, width), width)
            columns = []
            for lag in range(lags):
                pieces = []
                for block in range(TILE_BLOCKS):
                    source = first + (lead + block - lag)
                    kept = jnp.concatenate([live[first + block, lag]] * (width // live.shape[2]), axis=0)
                    pieces.append(arrived[chunk, source, channels, :] * kept)
                columns.append(jnp.concatenate(pieces, axis=0))
            window = jnp.concatenate(columns, axis=1)
            conv = jnp.dot(
                window, toeplitz[chunk * chunk_groups + group], preferred_element_type=jnp.float32
            )
            skip_row = part * share + chunk * rows + group * width
            skip = skips[pl.ds(pl.multiple_of(skip_row, width), width), :]
            for block in range(TILE_BLOCKS):
                direct = arrived[chunk, first + (lead + block), channels, :].astype(jnp.float32)
                total = conv[block * width : (block + 1) * width] + skip * direct
                mixed[chunk, first + block, channels, :] = total.astype(jnp.bfloat16)

        back[chunk, me] = mixed[chunk, me]

        @pl.loop(1, n)
        def _(k, chunk=chunk):
            copy_back(chunk, peer(k), me).start()

    def finish(lanes, turned):
        product = turned.astype(jnp.float32).T * post[:, lanes].astype(jnp.float32)
        out_ref[:, lanes] = product.astype(jnp.bfloat16)

    joint = max(BLK // rows, 1)
    if share % BLK == 0:
        for first in range(0, chunks, joint):

            @pl.loop(0, n)
            def _(k, first=first):
                device = peer(k)

                @pl.when(k > 0)
                def _():
                    for chunk in range(first, first + joint):
                        copy_back(chunk, me, device).wait_recv()

                pieces = [back[chunk, device] for chunk in range(first, first + joint)]
                lane = slab_of(device) * share + first * rows
                finish(pl.ds(pl.multiple_of(lane, BLK), joint * rows), jnp.concatenate(pieces, axis=0))

    else:

        @pl.loop(1, n)
        def _(k):
            copy_back(0, me, peer(k)).wait_recv()

        @pl.loop(0, n // joint)
        def _(tile):
            slabs = [tile * joint + index for index in range(joint)]
            pieces = [back[0, lax.rem(slab, stretch) * ctx + slab // stretch] for slab in slabs]
            finish(pl.ds(pl.multiple_of(tile * BLK, BLK), BLK), jnp.concatenate(pieces, axis=0))

    for chunk in range(chunks):

        @pl.loop(1, n)
        def _(k, chunk=chunk):
            copy_in(chunk, peer(k), me).wait_send()
            copy_back(chunk, peer(k), me).wait_send()


def per_device(stretch, ctx, post_gate, pre_gate, values, filters, skip_bias, doc_blocks):
    n = stretch * ctx
    tok_rows, model = values.shape
    taps = filters.shape[1]
    share = model // n
    groups = filters.shape[0] // stretch
    width = share // groups
    blocks = n * tok_rows // BLK
    longest = blocks * 3 // 8
    lags = min(longest, taps // BLK + 1)
    chunks = share // BLK if share % BLK == 0 else 1
    rows = share // chunks
    slab = (chunks, n, rows, BLK)
    vmem = pl.BlockSpec(memory_space=pltpu.VMEM)
    sems = pltpu.SemaphoreType.DMA((chunks, n))
    return pl.pallas_call(
        functools.partial(kernel, stretch, ctx, chunks, lags, width),
        out_shape=jax.ShapeDtypeStruct((tok_rows, model), jnp.bfloat16),
        in_specs=[
            pl.BlockSpec(memory_space=pltpu.HBM),
            pl.BlockSpec(memory_space=pltpu.HBM),
            pl.BlockSpec(memory_space=pltpu.HBM),
            pl.BlockSpec(memory_space=pltpu.HBM),
            vmem,
            pl.BlockSpec(memory_space=pltpu.SMEM),
        ],
        out_specs=vmem,
        scratch_shapes=[
            pltpu.VMEM((tok_rows, model), jnp.bfloat16),
            pltpu.VMEM((tok_rows, model), jnp.bfloat16),
            pltpu.VMEM((tok_rows, model), jnp.bfloat16),
            pltpu.VMEM(filters.shape, jnp.float32),
            pltpu.VMEM(slab, jnp.bfloat16),
            pltpu.VMEM((chunks, lags - 1 + n, rows, BLK), jnp.bfloat16),
            pltpu.VMEM(slab, jnp.bfloat16),
            pltpu.VMEM(slab, jnp.bfloat16),
            pltpu.VMEM((groups, lags * BLK, BLK), jnp.bfloat16),
            pltpu.VMEM((stretch * share, BLK), jnp.float32),
            pltpu.VMEM((blocks, lags, 16, BLK), jnp.bfloat16),
            pltpu.SemaphoreType.DMA((4,)),
            sems, sems, sems, sems,
        ],
        compiler_params=pltpu.CompilerParams(
            collective_id=0, has_side_effects=True, vmem_limit_bytes=51 * 1024 * 1024
        ),
    )(pre_gate, values, post_gate, filters, skip_bias, doc_blocks)


def solution(mesh):
    rows = P(("stretch", "ctx"), None)
    body = functools.partial(per_device, mesh.shape["stretch"], mesh.shape["ctx"])
    return jax.shard_map(
        body,
        mesh=mesh,
        in_specs=(rows, rows, rows, P("ctx", None), P("ctx"), P()),
        out_specs=rows,
        check_vma=False,
    )
```

```python
import functools
import math

import jax
import jax.numpy as jnp
from jax import lax
from jax.experimental import pallas as pl
from jax.experimental.pallas import tpu as pltpu
from jax.sharding import PartitionSpec as P

BLK = 128
TILE_BLOCKS = 8
MESH = pl.DeviceIdType.MESH


def kernel(
    stretch, ctx, chunks, lags, width,
    pre_ref, val_ref, post_ref, filt_ref, skip_ref, docs_ref, out_ref,
    pre, val, post, filt, gated, arrived, mixed, back, toeplitz, skips, live,
    load_sem, send_in, recv_in, send_back, recv_back,
):
    loads = [
        pltpu.make_async_copy(pre_ref, pre, load_sem.at[0]),
        pltpu.make_async_copy(val_ref, val, load_sem.at[1]),
        pltpu.make_async_copy(filt_ref, filt, load_sem.at[2]),
        pltpu.make_async_copy(post_ref, post, load_sem.at[3]),
    ]
    for load in loads:
        load.start()
    part = lax.axis_index("stretch")
    n = stretch * ctx
    me = lax.axis_index("stretch") * ctx + lax.axis_index("ctx")
    rows = gated.shape[2]
    share = chunks * rows
    lead = lags - 1
    chunk_groups = rows // width
    stride = 3 if math.gcd(3, n) == 1 else 1

    def peer(k):
        return lax.rem(me + k * stride, n)

    def place(device):
        return (device // ctx, lax.rem(device, ctx))

    def slab_of(device):
        return lax.rem(device, ctx) * stretch + device // ctx

    barrier = pltpu.get_barrier_semaphore()

    @pl.loop(1, n)
    def _(k):
        pl.semaphore_signal(barrier, inc=1, device_id=place(peer(k)), device_id_type=MESH)

    def copy_in(chunk, device, slot):
        return pltpu.make_async_remote_copy(
            src_ref=gated.at[chunk, slab_of(device)],
            dst_ref=arrived.at[chunk, lead + slot],
            send_sem=send_in.at[chunk, device],
            recv_sem=recv_in.at[chunk, slot],
            device_id=place(device),
            device_id_type=MESH,
        )

    def copy_back(chunk, device, slot):
        return pltpu.make_async_remote_copy(
            src_ref=mixed.at[chunk, device],
            dst_ref=back.at[chunk, slot],
            send_sem=send_back.at[chunk, device],
            recv_sem=recv_back.at[chunk, slot],
            device_id=place(device),
            device_id_type=MESH,
        )

    unit = max(share, BLK)
    per_unit = unit // share

    def gate(tile):
        lanes = pl.ds(pl.multiple_of(tile * unit, unit), unit)
        product = pre[:, lanes].astype(jnp.float32) * val[:, lanes].astype(jnp.float32)
        turned = product.T.astype(jnp.bfloat16)
        for slab in range(per_unit):
            for chunk in range(chunks):
                first = slab * share + chunk * rows
                gated[chunk, tile * per_unit + slab] = turned[first : first + rows]

    for load in loads[:2]:
        load.wait()
    early = n // 4 if per_unit == 1 else n

    if per_unit == 1:

        @pl.loop(0, early)
        def _(k):
            gate(slab_of(peer(k)))

    else:

        @pl.loop(0, n // per_unit)
        def _(tile):
            gate(tile)

    pl.semaphore_wait(barrier, n - 1)

    @pl.loop(1, early)
    def _(k):
        copy_in(0, peer(k), me).start()

    @pl.loop(early, n)
    def _(k):
        gate(slab_of(peer(k)))
        copy_in(0, peer(k), me).start()

    for chunk in range(1, chunks):

        @pl.loop(1, n)
        def _(k, chunk=chunk):
            copy_in(chunk, peer(k), me).start()

    for chunk in range(chunks):
        arrived[chunk, lead + me] = gated[chunk, slab_of(me)]
        arrived[chunk, 0:lead] = jnp.zeros((lead, rows, BLK), jnp.bfloat16)

    loads[2].wait()
    loads[3].wait()
    taps = filt.shape[1]

    @pl.loop(0, chunks * chunk_groups)
    def _(group):
        row = part * (chunks * chunk_groups) + group
        chosen = lax.broadcasted_iota(jnp.int32, (filt.shape[0], BLK), 0) == row
        for lag in range(lags):
            pieces = []
            for first in ((lag - 1) * BLK, lag * BLK):
                if 0 <= first < taps:
                    picked = jnp.where(chosen, filt[:, first : first + BLK], 0.0)
                    pieces.append(jnp.sum(picked, axis=0, keepdims=True))
                else:
                    pieces.append(jnp.zeros((1, BLK), jnp.float32))
            spread = jnp.broadcast_to(jnp.concatenate(pieces, axis=1), (BLK, 2 * BLK))
            turned = pltpu.roll(spread, 0, 1, stride=1, stride_axis=0)
            toeplitz[group, lag * BLK : (lag + 1) * BLK, :] = turned[:, BLK:].astype(jnp.bfloat16)

    skips[...] = jnp.broadcast_to(skip_ref[...].reshape(1, stretch * share), (BLK, stretch * share)).T
    ends = []
    for doc in range(docs_ref.shape[0]):
        ends.append(docs_ref[doc] + (ends[-1] if ends else 0))

    @pl.loop(0, n)
    def _(block):
        start = jnp.int32(0)
        for end in ends:
            start = jnp.maximum(start, jnp.where(end <= block, end, 0))
        for lag in range(lags):
            weight = jnp.where(block - lag >= start, 1.0, 0.0).astype(jnp.float32)
            live[block, lag] = jnp.full(live.shape[2:], weight, jnp.float32).astype(jnp.bfloat16)

    for chunk in range(chunks):

        @pl.loop(1, n)
        def _(k, chunk=chunk):
            copy_in(chunk, me, peer(k)).wait_recv()

        @pl.loop(0, chunk_groups * (n // TILE_BLOCKS))
        def _(step, chunk=chunk):
            group = step // (n // TILE_BLOCKS)
            first = lax.rem(step, n // TILE_BLOCKS) * TILE_BLOCKS
            channels = pl.ds(pl.multiple_of(group * width, width), width)
            columns = []
            for lag in range(lags):
                pieces = []
                for block in range(TILE_BLOCKS):
                    source = first + (lead + block - lag)
                    kept = jnp.concatenate([live[first + block, lag]] * (width // live.shape[2]), axis=0)
                    pieces.append(arrived[chunk, source, channels, :] * kept)
                columns.append(jnp.concatenate(pieces, axis=0))
            window = jnp.concatenate(columns, axis=1)
            conv = jnp.dot(
                window, toeplitz[chunk * chunk_groups + group], preferred_element_type=jnp.float32
            )
            skip_row = part * share + chunk * rows + group * width
            skip = skips[pl.ds(pl.multiple_of(skip_row, width), width), :]
            for block in range(TILE_BLOCKS):
                direct = arrived[chunk, first + (lead + block), channels, :].astype(jnp.float32)
                total = conv[block * width : (block + 1) * width] + skip * direct
                mixed[chunk, first + block, channels, :] = total.astype(jnp.bfloat16)

        back[chunk, me] = mixed[chunk, me]

        @pl.loop(1, n)
        def _(k, chunk=chunk):
            copy_back(chunk, peer(k), me).start()

    def finish(lanes, turned):
        product = turned.astype(jnp.float32).T * post[:, lanes].astype(jnp.float32)
        out_ref[:, lanes] = product.astype(jnp.bfloat16)

    joint = max(BLK // rows, 1)
    if share % BLK == 0:
        for first in range(0, chunks, joint):

            @pl.loop(0, n)
            def _(k, first=first):
                device = peer(k)

                @pl.when(k > 0)
                def _():
                    for chunk in range(first, first + joint):
                        copy_back(chunk, me, device).wait_recv()

                pieces = [back[chunk, device] for chunk in range(first, first + joint)]
                lane = slab_of(device) * share + first * rows
                finish(pl.ds(pl.multiple_of(lane, BLK), joint * rows), jnp.concatenate(pieces, axis=0))

    else:

        @pl.loop(1, n)
        def _(k):
            copy_back(0, me, peer(k)).wait_recv()

        @pl.loop(0, n // joint)
        def _(tile):
            slabs = [tile * joint + index for index in range(joint)]
            pieces = [back[0, lax.rem(slab, stretch) * ctx + slab // stretch] for slab in slabs]
            finish(pl.ds(pl.multiple_of(tile * BLK, BLK), BLK), jnp.concatenate(pieces, axis=0))

    for chunk in range(chunks):

        @pl.loop(1, n)
        def _(k, chunk=chunk):
            copy_in(chunk, peer(k), me).wait_send()
            copy_back(chunk, peer(k), me).wait_send()


def per_device(stretch, ctx, post_gate, pre_gate, values, filters, skip_bias, doc_blocks):
    n = stretch * ctx
    tok_rows, model = values.shape
    taps = filters.shape[1]
    share = model // n
    groups = filters.shape[0] // stretch
    width = share // groups
    blocks = n * tok_rows // BLK
    longest = blocks * 3 // 8
    lags = min(longest, taps // BLK + 1)
    chunks = share // BLK if share % BLK == 0 else 1
    rows = share // chunks
    slab = (chunks, n, rows, BLK)
    vmem = pl.BlockSpec(memory_space=pltpu.VMEM)
    sems = pltpu.SemaphoreType.DMA((chunks, n))
    return pl.pallas_call(
        functools.partial(kernel, stretch, ctx, chunks, lags, width),
        out_shape=jax.ShapeDtypeStruct((tok_rows, model), jnp.bfloat16),
        in_specs=[
            pl.BlockSpec(memory_space=pltpu.HBM),
            pl.BlockSpec(memory_space=pltpu.HBM),
            pl.BlockSpec(memory_space=pltpu.HBM),
            pl.BlockSpec(memory_space=pltpu.HBM),
            vmem,
            pl.BlockSpec(memory_space=pltpu.SMEM),
        ],
        out_specs=vmem,
        scratch_shapes=[
            pltpu.VMEM((tok_rows, model), jnp.bfloat16),
            pltpu.VMEM((tok_rows, model), jnp.bfloat16),
            pltpu.VMEM((tok_rows, model), jnp.bfloat16),
            pltpu.VMEM(filters.shape, jnp.float32),
            pltpu.VMEM(slab, jnp.bfloat16),
            pltpu.VMEM((chunks, lags - 1 + n, rows, BLK), jnp.bfloat16),
            pltpu.VMEM(slab, jnp.bfloat16),
            pltpu.VMEM(slab, jnp.bfloat16),
            pltpu.VMEM((groups, lags * BLK, BLK), jnp.bfloat16),
            pltpu.VMEM((stretch * share, BLK), jnp.float32),
            pltpu.VMEM((blocks, lags, 16, BLK), jnp.bfloat16),
            pltpu.SemaphoreType.DMA((4,)),
            sems, sems, sems, sems,
        ],
        compiler_params=pltpu.CompilerParams(
            collective_id=0, has_side_effects=True, vmem_limit_bytes=51 * 1024 * 1024
        ),
    )(pre_gate, values, post_gate, filters, skip_bias, doc_blocks)


def solution(mesh):
    rows = P(("stretch", "ctx"), None)
    body = functools.partial(per_device, mesh.shape["stretch"], mesh.shape["ctx"])
    return jax.shard_map(
        body,
        mesh=mesh,
        in_specs=(rows, rows, rows, P("ctx", None), P("ctx"), P()),
        out_specs=rows,
        check_vma=False,
    )
```
